512 devices in a mesh: dp: 8 (over x, core), mem: 64 (over z, y).
Axes of the slice: x: 4, y: 4, z: 16, core: 2. Of those that a mesh axis runs over, the one named last changes fastest.
Arguments:
- lookup_slot: int32 [65536, 4, 32], P(('dp', 'mem')), may hold values from 0 to 511
- lookup_weight: float32 [65536, 4, 32], P(('dp', 'mem')), may hold values from 0.02 to 0.3
- owner_route: int32 [65536, 2], P(('dp', 'mem')), may hold values from 0 to 63, all different within a row; in each aligned block of 128 rows (0 to 127, 128 to 255, ...) at most 8 rows name the same one
- values: bfloat16 [16384, 4096], P('mem'), may hold values from -1.5 to 1.5
- out_grad: bfloat16 [65536, 4096], P(('dp', 'mem')), may hold values from -0.3984375 to 0.3984375
Outputs:
- memory_out: bfloat16 [65536, 4096], P(('dp', 'mem'))
- grad_values: float32 [16384, 4096], P('mem', 'dp')
- grad_weight: float32 [65536, 4, 32], P(('dp', 'mem'))
The draws below stay inside these ranges and needn't reach their ends.
Inputs may be any that keep to these rules, and one draw needn't show every extreme that they name: `owner_route`: each row names 2 different owners; among the rows of one device no owner is named more than 8 times, a bound that some block reaches.
All inputs are finite; a program needn't handle non-finite values.
Results may differ from the reference program's by a relative error of at most 0.006.
Values may be sent and summed in bfloat16 or wider, within the bound.
A program may use at most 64 MiB of HBM per device.

```python
import math
import jax
import jax.numpy as jnp
import numpy as np
from jax import lax

D = 4096
H = 4
K = 32
G = 2
VAL_DEV = 256
TOK_DEV = 128
OWNERS = 64
TCAP = 8
VALUES = 16384
TOKENS = 65536


def set_ends(values, stream_key, least, high):
    index_at = [jax.random.randint(jax.random.fold_in(stream_key, axis), (), 0, length) for axis, length in enumerate(values.shape)]
    main_axis = values.shape.index(max(values.shape))
    beside = index_at[:main_axis] + [(index_at[main_axis] + 1) % values.shape[main_axis]] + index_at[main_axis + 1:]
    return values.at[tuple(index_at)].set(least).at[tuple(beside)].set(high)


def level_of(rng, dims, pieces, least, largest):
    def one(axis_at, blocks):
        draws = jax.random.uniform(jax.random.fold_in(jax.random.fold_in(rng, 6), axis_at), (blocks,), jnp.float32, least / len(pieces), largest / len(pieces))
        return jnp.repeat(jnp.exp(draws), dims[axis_at] // blocks).reshape((-1,) + (1,) * (len(dims) - axis_at - 1))

    factor_of = one(*pieces[0])
    for cut in pieces[1:]:
        factor_of = factor_of * one(*cut)
    return factor_of


def deal_out(own_key, own, number, rows, number_of, top, reach, slope):
    order = jax.random.permutation(own_key, number_of)
    crowded, ordinary = portions_of(number_of, rows * top, reach, slope, True), portions_of(number_of, rows * top, reach, slope, False)
    places = jnp.arange(number_of)

    def named(tallies, turn):
        used = int((tallies > 0).sum())
        fixed = max(1, used // 4)
        shifted = fixed + (places - fixed + turn * (used - fixed)) % max(1, number_of - fixed)
        return jnp.zeros((number_of,), jnp.int32).at[order[jnp.where(places < fixed, places, shifted)]].set(jnp.asarray(tallies, jnp.int32))

    tallies = jnp.where(number % 4 == 0, named(crowded, number // 4), named(ordinary, number - number // 4 - 1))
    mixed = jax.random.permutation(jax.random.fold_in(own, 3), number_of)
    source_of, sink = mixed[0:number_of // 2 * 2:2], mixed[1:number_of // 2 * 2:2]
    room = jnp.minimum(tallies[source_of] - 1, reach - tallies[sink]) // 2
    room = jnp.where((source_of == order[0]) | (sink == order[0]) | (tallies[sink] == 0), 0, jnp.maximum(room, 0))
    shifted = jax.random.randint(jax.random.fold_in(own, 4), (number_of // 2,), 0, 1 << 20) % (room + 1)
    tallies = tallies.at[source_of].add(-shifted).at[sink].add(shifted)
    members = jnp.searchsorted(jnp.cumsum(tallies), jnp.arange(rows * top), side="right").astype(jnp.int32)
    listing = members.reshape(top, rows).T
    listing = listing[jax.random.permutation(jax.random.fold_in(own, 1), rows)]
    turn = jax.random.randint(jax.random.fold_in(own, 2), (rows, 1), 0, top)
    return jnp.take_along_axis(listing, (jnp.arange(top)[None, :] + turn) % top, axis=1)


def portions_of(count, total, reach, lean, full):
    loads = [(1 << 20) // math.isqrt(rank ** lean) + 1 for rank in range(1, count + 1)]
    largest = reach if full else min(reach, max(-(-total // count), total * loads[0] // sum(loads)))
    least = 1 if total - largest >= count - 1 else 0
    holding, spare = [largest] + [least] * (count - 1), total - largest - least * (count - 1)
    while spare > 0:
        candidates = [i for i in range(1, count) if holding[i] < largest] or [i for i in range(1, count) if holding[i] < reach]
        pool, remaining = sum([loads[i] for i in candidates]), spare
        for i in candidates:
            extra = min(reach - holding[i], max(1, remaining * loads[i] // pool), spare)
            holding[i] = holding[i] + extra
            spare = spare - extra
    return np.array(holding)


def noise(stream_key, dims, deviation, limit, shards=(), kind=jnp.bfloat16):
    result = deviation * jax.random.normal(stream_key, dims, jnp.float32)
    if shards:
        result = result * level_of(stream_key, dims, shards, -0.22, 0.18)
    return jnp.clip(result, -limit, limit).astype(kind)


def setup_inputs(seed: int = 0) -> dict:
    arg_keys = jax.random.split(jax.random.key(seed), 6)
    lookup_slot = set_ends(jax.random.randint(arg_keys[0], (TOKENS, H, K), 0, G * VAL_DEV), jax.random.fold_in(arg_keys[0], 1), 0, (G * VAL_DEV) - 1).astype(jnp.int32)
    lookup_weight = jnp.clip(jnp.exp(math.log(0.3) - 2.7080503 * jax.random.uniform(arg_keys[1], (TOKENS, H, K), jnp.float32) ** level_of(arg_keys[1], (TOKENS, H, K), ((0, 512),), -0.2, 0.2)), 0.02, 0.3)
    owner_route_keys = jax.random.split(jax.random.fold_in(arg_keys[2], 1), TOKENS // TOK_DEV)
    owner_route_turns = jax.random.permutation(jax.random.fold_in(arg_keys[2], 3), TOKENS // TOK_DEV)
    owner_route = jax.vmap(lambda own, number: deal_out(jax.random.fold_in(arg_keys[2], 2), own, number, TOK_DEV, OWNERS, G, TCAP, 2))(owner_route_keys, owner_route_turns).reshape((TOKENS, G))
    values = noise(arg_keys[3], (VALUES, D), 0.25, 1.5, ((0, 64),))
    out_grad = noise(arg_keys[4], (TOKENS, D), 0.0625, 0.3984375, ((0, 512),))
    return {"lookup_slot": lookup_slot, "lookup_weight": lookup_weight, "owner_route": owner_route, "values": values, "out_grad": out_grad}


def reference(lookup_slot, lookup_weight, owner_route, values, out_grad):
    token_total = lookup_slot.shape[0]
    group_count = owner_route.shape[1]
    row_count = VAL_DEV
    pair_total = token_total * group_count
    flat_slot = lookup_slot.reshape(token_total, -1)
    flat_weight = lookup_weight.reshape(token_total, -1)
    token_ids = jnp.arange(token_total, dtype=jnp.int32)[:, None]
    dense_rows = jnp.zeros((token_total, group_count * row_count), jnp.float32).at[token_ids, flat_slot].add(flat_weight)
    dense_rows = dense_rows.astype(jnp.bfloat16).reshape(pair_total, row_count)
    dense_pad = jnp.concatenate([dense_rows, jnp.zeros((1, row_count), jnp.bfloat16)], axis=0)
    grad_pad = jnp.concatenate([out_grad, jnp.zeros((1, D), jnp.bfloat16)], axis=0)
    pair_owner = owner_route.reshape(pair_total)
    capacity = token_total // TOK_DEV * TCAP
    pair_ids = jnp.arange(pair_total, dtype=jnp.int32)
    highest = lax.Precision.HIGHEST

    def per_owner(scan_carry, owner_index):
        mixed_acc, pair_grad = scan_carry
        chosen = pair_owner == owner_index
        pair_rank = jnp.cumsum(chosen.astype(jnp.int32)) - 1
        target = jnp.where(chosen, pair_rank, capacity).astype(jnp.int32)
        slot_table = jnp.full((capacity + 1,), pair_total, jnp.int32).at[target].set(pair_ids)[:capacity]
        slot_weight = dense_pad[slot_table].astype(jnp.float32)
        slot_token = slot_table // group_count
        slot_grad = grad_pad[slot_token].astype(jnp.float32)
        value_block = lax.dynamic_slice_in_dim(values, (owner_index * row_count).astype(jnp.int32), row_count, 0).astype(jnp.float32)
        partial_value = jnp.dot(slot_weight, value_block, precision=highest).astype(jnp.bfloat16)
        partial_value = lax.optimization_barrier(partial_value).astype(jnp.float32)
        mixed_acc = mixed_acc.at[slot_token].add(partial_value, mode="drop")
        value_grad = jnp.dot(slot_weight.T, slot_grad, precision=highest)
        slot_product = jnp.dot(slot_grad, value_block.T, precision=highest)
        pair_grad = pair_grad.at[slot_table].set(slot_product, mode="drop")
        return (mixed_acc, pair_grad), value_grad

    start_carry = (jnp.zeros((token_total, D), jnp.float32), jnp.zeros((pair_total, row_count), jnp.float32))
    final_carry, value_grads = lax.scan(per_owner, start_carry, jnp.arange(OWNERS, dtype=jnp.int32))
    mixed_acc, pair_grad = final_carry
    memory_out = mixed_acc.astype(jnp.bfloat16)
    grad_values = value_grads.reshape(OWNERS * row_count, D)
    grad_weight = jnp.take_along_axis(pair_grad.reshape(token_total, group_count * row_count), flat_slot, axis=1)
    return memory_out, grad_values, grad_weight.reshape(lookup_slot.shape)
```

```python
import functools

import jax
import jax.numpy as jnp
from jax import lax
from jax.experimental import pallas as pl
from jax.experimental.pallas import tpu as pltpu
from jax.sharding import PartitionSpec as P

MESH = pl.DeviceIdType.MESH
X, K, Z, Y = 4, 2, 16, 4
C = X * K
TOK, PICKS, ROWS, FEAT, CAP = 128, 128, 256, 512, 8
HALF = ROWS // 2
SLOTS = Z * CAP
MSG = SLOTS + 16
F32, BF16 = jnp.float32, jnp.bfloat16
NT = (((1,), (1,)), ((), ()))
TN = (((0,), (0,)), ((), ()))


class Ids:
    def __init__(self):
        self.count = 0

    def take(self, number=1):
        first = self.count
        self.count += number
        return first


def exchange(
    slot_t, weight_t, place, og, values,
    out, gv, pair,
    va, oga, wm, wa, ps, dense_t, pm, wt, gt, pt, ip, ir, ic, ix, iy, isrc,
    outp, ytr, ytl, yfr, yfl, rz, sz, ssem, rsem, lsem,
):
    dp, mem = lax.axis_index("dp"), lax.axis_index("mem")
    x, k = dp // K, dp % K
    z, y = mem // Y, mem % Y
    ids = Ids()
    sent = []

    def dev(dx=0, dk=0, dz=0, dy=0):
        to_dp = ((x + dx) % X) * K + (k + dk) % K
        to_mem = ((z + dz) % Z) * Y + (y + dy) % Y
        return (to_dp, to_mem)

    def cof(dx, dk):
        return ((x + dx) % X) * K + (k + dk) % K

    def copy(src, dst, sem, to):
        return pltpu.make_async_remote_copy(
            src_ref=src, dst_ref=dst, send_sem=ssem.at[sem], recv_sem=rsem.at[sem],
            device_id=to, device_id_type=MESH,
        )

    def send(src, dst, sem, to):
        one = copy(src, dst, sem, to)
        one.start()
        sent.append(one)

    def arrived(dst, sem):
        copy(dst, dst, sem, dev(dk=1)).wait_recv()

    def cols(index):
        return pl.ds(pl.multiple_of(index * FEAT, FEAT), FEAT)

    c = dp
    own_v = [
        pltpu.make_async_copy(
            values.at[pl.ds(h * HALF, HALF), cols(c)], va.at[z, h], lsem.at[h]
        )
        for h in range(2)
    ]
    for one in own_v:
        one.start()
    own_og = pltpu.make_async_copy(og.at[:, cols(c)], oga.at[c, y], lsem.at[2])
    own_og.start()

    barrier = pltpu.get_barrier_semaphore()
    others = [(dx, dk) for dx in range(X) for dk in range(K) if (dx, dk) != (0, 0)]
    partners = [dev(dz=1), dev(dz=Z - 1)] + [dev(dy=d) for d in range(1, Y)]
    partners += [dev(dx=dx, dk=dk) for dx, dk in others]
    for partner in partners:
        pl.semaphore_signal(barrier, inc=1, device_id=partner, device_id_type=MESH)
    pl.semaphore_wait(barrier, len(partners))

    hops = {("r", 0): 8, ("r", 1): 7, ("l", 0): 7, ("l", 1): 8}
    zid = {(key, s): ids.take() for key, n in hops.items() for s in range(1, n + 1)}

    def z_send(s):
        for (way, h), n in hops.items():
            if s <= n:
                if way == "r":
                    at, to = (z + Z - s + 1) % Z, dev(dz=1)
                else:
                    at, to = (z + s - 1) % Z, dev(dz=Z - 1)
                send(va.at[at, h], va.at[at, h], zid[((way, h), s)], to)

    def z_wait(s):
        for (way, h), n in hops.items():
            if s <= n:
                at = (z + Z - s) % Z if way == "r" else (z + s) % Z
                arrived(va.at[at, h], zid[((way, h), s)])

    def z_step(s):
        z_wait(s)
        if s < 8:
            z_send(s + 1)

    order = [(0, 0), (0, 1), (1, 0), (1, 1), (3, 0), (3, 1), (2, 0), (2, 1)]
    cid = [ids.take() for _ in order]
    yr1 = [ids.take() for _ in order]
    yl1 = [ids.take() for _ in order]
    y2 = [ids.take() for _ in order]

    def c_send(i):
        dx, dk = order[i]
        to = cof(dx, dk)
        send(og.at[:, cols(to)], oga.at[c, y], cid[i], dev(dx=dx, dk=dk))

    def source(i):
        dx, dk = order[i]
        return cof(X - dx, dk)

    def y_send(i):
        block = oga.at[source(i), y]
        send(block, block, yr1[i], dev(dy=1))
        send(block, block, yl1[i], dev(dy=Y - 1))

    def c_step(i):
        arrived(oga.at[source(i), y], cid[i])
        y_send(i)

    def y_step(i):
        right = oga.at[source(i), (y + Y - 1) % Y]
        left = oga.at[source(i), (y + 1) % Y]
        arrived(right, yr1[i])
        arrived(left, yl1[i])
        if i % 2 == 0:
            send(right, right, y2[i], dev(dy=1))
        else:
            send(left, left, y2[i], dev(dy=Y - 1))

    def y_last(i):
        arrived(oga.at[source(i), (y + 2) % Y], y2[i])

    w1 = [ids.take() for _ in range(3)]
    w2 = [ids.take() for _ in range(4)]
    w3 = [ids.take() for _ in range(4)]

    for one in own_v:
        one.wait()
    z_send(1)
    for i in range(1, 8):
        c_send(i)
    own_og.wait()
    y_send(0)
    c_step(1)

    for a in range(4):
        columns = lax.broadcasted_iota(jnp.int32, (128, TOK), 0) + a * 128

        def spread(step, total):
            at = pl.multiple_of(step * 8, 8)
            slot_rows, weight_rows = slot_t[pl.ds(at, 8), :], weight_t[pl.ds(at, 8), :]
            for u in range(8):
                hit = columns == slot_rows[u : u + 1, :]
                total = total + jnp.where(hit, weight_rows[u : u + 1, :], 0.0)
            return total

        total = lax.fori_loop(0, PICKS // 8, spread, jnp.zeros((128, TOK), F32))
        dense_t[pl.ds(a * 128, 128), :] = total.astype(BF16)

    slot_ids = lax.broadcasted_iota(jnp.int32, (SLOTS, TOK), 0)
    for to in range(Y):
        total = jnp.zeros((SLOTS, ROWS), F32)
        lanes = []
        for j in range(2):
            row = place[pl.ds(to * 2 + j, 1), :]
            one = jnp.where(slot_ids == row, 1.0, 0.0).astype(BF16)
            ps[j, pl.ds(to * SLOTS, SLOTS), :] = one
            total = total + lax.dot_general(
                one, dense_t[pl.ds(j * ROWS, ROWS), :], NT, preferred_element_type=F32
            )
            lanes.append(place[pl.ds(8 + to * 2 + j, 1), :].astype(F32))
        wm[to, pl.ds(0, SLOTS), :] = total.astype(BF16)
        wm[to, pl.ds(SLOTS, 16), :] = jnp.broadcast_to(
            jnp.concatenate(lanes, axis=1), (16, ROWS)
        ).astype(BF16)
    for i in range(3):
        send(wm.at[(y + i + 1) % Y], wa.at[c, y], w1[i], dev(dy=i + 1))
    wa[c, y] = wm[y]

    z_step(1)
    for i in (2, 3, 4, 5):
        c_step(i)
    for i in range(3):
        arrived(wa.at[c, (y + Y - i - 1) % Y], w1[i])
    send(wa.at[c], wa.at[c], w2[0], dev(dk=1))
    for dx in (1, 3, 2):
        send(wa.at[c], wa.at[c], w2[dx], dev(dx=dx))
    z_step(2)
    for i in (6, 7):
        c_step(i)
    y_step(0)
    y_step(1)
    z_step(3)
    arrived(wa.at[cof(0, 1)], w2[0])
    for dx in (1, 3, 2):
        block = wa.at[cof(X - dx, 0)]
        arrived(block, w2[dx])
        send(block, block, w3[dx], dev(dk=1))
    y_step(2)
    y_step(3)
    z_step(4)
    y_step(4)
    y_step(5)
    z_step(5)
    for dx in (1, 3, 2):
        arrived(wa.at[cof(X - dx, 1)], w3[dx])

    def prepare(pi, carry):
        kk, xx, yp = pi // 8, (pi // 2) % 4, pi % 2
        src = xx * K + kk
        slots = lax.broadcasted_iota(jnp.int32, (ROWS, TOK), 0).astype(F32)
        at = pl.multiple_of(pi * 16, 16)
        parts = []
        for q in range(2):
            row = wa[src, yp * 2 + q, pl.ds(SLOTS, 16), :].astype(F32)[0:1, :]
            hit = jnp.where(slots == row[:, :TOK], 1.0, 0.0)
            hit = hit + jnp.where(slots == row[:, TOK:], 1.0, 0.0)
            pm[pi, :, pl.ds(q * TOK, TOK)] = hit.astype(BF16)
            part = wa[src, yp * 2 + q, pl.ds(0, SLOTS), :].astype(F32)
            parts.append(part.reshape(Z, CAP, ROWS))
        both = jnp.concatenate(parts, axis=1)
        wt[:, pl.ds(at, 16), :] = both.astype(BF16)
        return carry

    lax.fori_loop(0, 16, prepare, 0)
    y_step(6)
    y_step(7)
    z_step(6)
    z_step(7)
    for i in range(8):
        y_last(i)

    def gather(pi, carry):
        kk, xx, yp = pi // 8, (pi // 2) % 4, pi % 2
        src = xx * K + kk
        at = pl.multiple_of(pi * 16, 16)
        tokens = oga[src, pl.ds(yp * 2, 2)].reshape(2 * TOK, FEAT)
        got = jnp.dot(pm[pi], tokens, preferred_element_type=F32)
        gt[:, pl.ds(at, 16), :] = got.astype(BF16).reshape(Z, 16, FEAT)
        return carry

    lax.fori_loop(0, 16, gather, 0)

    rid = ids.take(32)

    def grad_part(at, h):
        rows = pl.ds(pl.multiple_of(h * HALF, HALF), HALF)
        return lax.dot_general(wt[at, :, rows], gt[at], TN, preferred_element_type=F32)

    def r_step(s):
        def stream(u, carry):
            way, h = (u, u) if s == 0 else (u // 2, u % 2)
            at = (z + Z + (1 - 2 * way) * (8 - s)) % Z
            total = grad_part(at, h)
            if s >= 1:
                before = rid + (s - 1) * 4 + way * 2 + h
                if s == 1:
                    total_ref = sz.at[s, way, h]

                    @pl.when(way == h)
                    def _():
                        arrived(rz.at[s - 1, way, h], before)
                        got = total + rz[s - 1, way, h].astype(F32)
                        total_ref[...] = got.astype(BF16)

                    @pl.when(way != h)
                    def _():
                        total_ref[...] = total.astype(BF16)

                else:
                    arrived(rz.at[s - 1, way, h], before)
                    total = total + rz[s - 1, way, h].astype(F32)
                    sz[s, way, h] = total.astype(BF16)
            else:
                sz[s, way, h] = total.astype(BF16)
            to_mem = ((z + Z + 1 - 2 * way) % Z) * Y + y
            copy(
                sz.at[s, way, h], rz.at[s, way, h], rid + s * 4 + way * 2 + h, (dp, to_mem)
            ).start()
            return carry

        lax.fori_loop(0, 2 if s == 0 else 4, stream, 0)

    def r_last():
        def finish(h, carry):
            total = grad_part(z, h)
            for way in range(2):
                arrived(rz.at[7, way, h], rid + 28 + way * 2 + h)
                total = total + rz[7, way, h].astype(F32)
            gv[pl.ds(pl.multiple_of(h * HALF, HALF), HALF), :] = total
            return carry

        lax.fori_loop(0, 2, finish, 0)

        def drain(i, carry):
            s, u = i // 4, i % 4

            @pl.when((i != 1) & (i != 2))
            def _():
                copy(sz.at[s, u // 2, u % 2], sz.at[s, u // 2, u % 2], rid + i, dev(dz=1)).wait_send()

            return carry

        lax.fori_loop(0, 32, drain, 0)

    r_step(0)
    z_wait(8)

    def multiply(at, carry):
        rows = va[at].reshape(ROWS, FEAT)
        pt[at] = jnp.dot(wt[at], rows, preferred_element_type=F32).astype(BF16)
        inner = lax.dot_general(gt[at], rows, NT, preferred_element_type=F32)
        ip[:, :, at] = inner.astype(BF16).reshape(K, X, 32, ROWS)
        return carry

    lax.fori_loop(0, Z, multiply, 0)
    i1 = ids.take()
    i2 = [ids.take() for _ in range(4)]
    i3 = [ids.take() for _ in range(4)]
    send(ip.at[(k + 1) % K], ir, i1, dev(dk=1))

    def scatter(pi, carry):
        kk, xx, yp = pi // 8, (pi // 2) % 4, pi % 2
        src = xx * K + kk
        at = pl.multiple_of(pi * 16, 16)
        parts = pt[:, pl.ds(at, 16), :].reshape(ROWS, FEAT)
        got = lax.dot_general(pm[pi], parts, TN, preferred_element_type=F32)
        outp[src, pl.ds(yp * 2, 2)] = got.astype(BF16).reshape(2, TOK, FEAT)
        return carry

    lax.fori_loop(0, 16, scatter, 0)

    m1 = [ids.take() for _ in range(8)]
    mr = [ids.take() for _ in range(8)]
    ml = [ids.take() for _ in range(8)]
    oid = [ids.take() for _ in order]
    far, up, down = (y + 2) % Y, (y + 1) % Y, (y + Y - 1) % Y
    for i in range(4):
        send(outp.at[i, far], ytr.at[i], m1[i], dev(dy=1))
        send(outp.at[i + 4, far], ytl.at[i], m1[i + 4], dev(dy=Y - 1))
    for i in range(4):
        send(outp.at[i + 4, up], yfr.at[i + 4], mr[i + 4], dev(dy=1))
        send(outp.at[i, down], yfl.at[i], ml[i], dev(dy=Y - 1))

    def m_step(i):
        arrived(ytr.at[i], m1[i])
        outp[i, up] = (outp[i, up].astype(F32) + ytr[i].astype(F32)).astype(BF16)
        send(outp.at[i, up], yfr.at[i], mr[i], dev(dy=1))
        arrived(ytl.at[i], m1[i + 4])
        outp[i + 4, down] = (outp[i + 4, down].astype(F32) + ytl[i].astype(F32)).astype(BF16)
        send(outp.at[i + 4, down], yfl.at[i + 4], ml[i + 4], dev(dy=Y - 1))

    def f_wait(i):
        arrived(yfr.at[i], mr[i])
        arrived(yfl.at[i], ml[i])

    def f_send(i):
        dx, dk = order[i]
        to = cof(dx, dk)
        total = outp[to, y].astype(F32) + yfr[to].astype(F32) + yfl[to].astype(F32)
        outp[to, y] = total.astype(BF16)
        if i == 0:
            own = pltpu.make_async_copy(outp.at[to, y], out.at[:, cols(c)], lsem.at[3])
            own.start()
            own.wait()
        else:
            send(outp.at[to, y], out.at[:, cols(c)], oid[i], dev(dx=dx, dk=dk))

    r_step(1)
    arrived(ir, i1)

    def add_core(i, carry):
        xx = i // 4
        at = pl.ds((i % 4) * 4, 4)
        ic[xx, at] = (ip[k, xx, at].astype(F32) + ir[xx, at].astype(F32)).astype(BF16)
        return carry

    lax.fori_loop(0, 16, add_core, 0)
    for dx in (1, 3, 2):
        send(ic.at[(x + dx) % X], ix.at[dx - 1], i2[dx], dev(dx=dx))
    m_step(0)
    r_step(2)
    m_step(1)
    m_step(2)
    r_step(3)
    m_step(3)
    for dx in (1, 3, 2):
        arrived(ix.at[dx - 1], i2[dx])

    def add_chips(at, carry):
        total = ic[x, at].astype(F32)
        for i in range(3):
            total = total + ix[i, at].astype(F32)
        for q in range(4):
            iy[q, at] = total[q * CAP : (q + 1) * CAP, :]
        return carry

    lax.fori_loop(0, Z, add_chips, 0)
    for q in range(4):
        isrc[4, pl.ds(q * SLOTS, SLOTS), :] = iy[q].reshape(SLOTS, ROWS).astype(BF16)
    isrc[0, pl.ds(0, SLOTS), :] = isrc[4, pl.ds(pl.multiple_of(y * SLOTS, SLOTS), SLOTS), :]
    for i in range(1, 4):
        to = (y + i) % Y
        send(
            isrc.at[4, pl.ds(pl.multiple_of(to * SLOTS, SLOTS), SLOTS), :],
            isrc.at[i, pl.ds(0, SLOTS), :], i3[i], dev(dy=i),
        )
    r_step(4)
    r_step(5)
    for i in range(1, 4):
        arrived(isrc.at[i, pl.ds(0, SLOTS), :], i3[i])
    for j in range(2):
        total = jnp.zeros((TOK, ROWS), F32)
        for i in range(4):
            at = pl.multiple_of(((y + Y - i) % Y) * SLOTS, SLOTS)
            total = total + lax.dot_general(
                ps[j, pl.ds(at, SLOTS), :], isrc[i, pl.ds(0, SLOTS), :], TN,
                preferred_element_type=F32,
            )
        pair[:, pl.ds(j * ROWS, ROWS)] = total
    r_step(6)
    for i in range(8):
        f_wait(i)
    for i in (6, 7, 2, 3, 4, 5, 1, 0):
        f_send(i)
    r_step(7)
    r_last()
    for i in range(1, 8):
        arrived(out.at[:, cols(source(i))], oid[i])
    for one in sent:
        one.wait_send()
    assert ids.count <= SEMS, ids.count


SEMS = 160


def pick(pair_ref, slot_ref, out_ref):
    slot = slot_ref[...]
    low, high = slot & 127, slot // 128
    total = jnp.zeros((TOK, PICKS), F32)
    for a in range(4):
        part = jnp.take_along_axis(pair_ref[:, pl.ds(a * 128, 128)], low, axis=1)
        total = jnp.where(high == a, part, total)
    out_ref[...] = total


def shards(lookup_slot, lookup_weight, owner_route, values, out_grad):
    y = lax.axis_index("mem") % Y
    flat_slot = lookup_slot.reshape(TOK, PICKS)
    flat_weight = lookup_weight.reshape(TOK, PICKS)
    owner = owner_route.T.reshape(2 * TOK)
    number = jnp.arange(2 * TOK, dtype=jnp.int32)
    earlier = (owner[:, None] == owner[None, :]) & (number[:, None] < number[None, :])
    rank = jnp.sum(earlier.astype(jnp.int32), axis=0)
    slot = (owner // Y) * CAP + rank
    wide = (owner // Y) * (2 * CAP) + rank + (y % 2) * CAP
    here = (owner % Y)[None, :] == jnp.arange(Y, dtype=jnp.int32)[:, None]
    place = jnp.concatenate(
        [
            jnp.where(here, slot[None, :], -1).reshape(2 * Y, TOK),
            jnp.where(here, wide[None, :], -1).reshape(2 * Y, TOK),
        ]
    )
    vmem, anywhere = pl.BlockSpec(memory_space=pltpu.VMEM), pl.BlockSpec(memory_space=pl.ANY)
    out, gv, pair = pl.pallas_call(
        exchange,
        out_shape=(
            jax.ShapeDtypeStruct((TOK, C * FEAT), BF16),
            jax.ShapeDtypeStruct((ROWS, FEAT), F32),
            jax.ShapeDtypeStruct((TOK, 2 * ROWS), F32),
        ),
        in_specs=[vmem, vmem, vmem, vmem, anywhere],
        out_specs=(vmem, vmem, vmem),
        scratch_shapes=[
            pltpu.VMEM((Z, 2, HALF, FEAT), BF16),
            pltpu.VMEM((C, Y, TOK, FEAT), BF16),
            pltpu.VMEM((Y, MSG, ROWS), BF16),
            pltpu.VMEM((C, Y, MSG, ROWS), BF16),
            pltpu.VMEM((2, Y * SLOTS, TOK), BF16),
            pltpu.VMEM((2 * ROWS, TOK), BF16),
            pltpu.VMEM((16, ROWS, 2 * TOK), BF16),
            pltpu.VMEM((Z, 16 * 16, ROWS), BF16),
            pltpu.VMEM((Z, 16 * 16, FEAT), BF16),
            pltpu.VMEM((Z, 16 * 16, FEAT), BF16),
            pltpu.VMEM((K, X, Z, 32, ROWS), BF16),
            pltpu.VMEM((X, Z, 32, ROWS), BF16),
            pltpu.VMEM((X, Z, 32, ROWS), BF16),
            pltpu.VMEM((3, Z, 32, ROWS), BF16),
            pltpu.VMEM((4, Z, CAP, ROWS), F32),
            pltpu.VMEM((5, Y * SLOTS, ROWS), BF16),
            pltpu.VMEM((C, Y, TOK, FEAT), BF16),
            pltpu.VMEM((4, TOK, FEAT), BF16),
            pltpu.VMEM((4, TOK, FEAT), BF16),
            pltpu.VMEM((C, TOK, FEAT), BF16),
            pltpu.VMEM((C, TOK, FEAT), BF16),
            pltpu.VMEM((8, 2, 2, HALF, FEAT), BF16),
            pltpu.VMEM((8, 2, 2, HALF, FEAT), BF16),
            pltpu.SemaphoreType.DMA((SEMS,)),
            pltpu.SemaphoreType.DMA((SEMS,)),
            pltpu.SemaphoreType.DMA((4,)),
        ],
        compiler_params=pltpu.CompilerParams(
            collective_id=0, has_side_effects=True, vmem_limit_bytes=58 * 1024 * 1024
        ),
        name="exchange",
    )(flat_slot.T, flat_weight.T, place, out_grad, values)
    grad_weight = pl.pallas_call(
        pick,
        out_shape=jax.ShapeDtypeStruct((TOK, PICKS), F32),
        in_specs=[vmem, vmem],
        out_specs=vmem,
        name="pick",
    )(pair, flat_slot)
    return out, gv, grad_weight.reshape(lookup_slot.shape)


def solution(mesh):
    return jax.shard_map(
        shards,
        mesh=mesh,
        in_specs=(
            P(("dp", "mem"), None, None),
            P(("dp", "mem"), None, None),
            P(("dp", "mem"), None),
            P("mem", None),
            P(("dp", "mem"), None),
        ),
        out_specs=(P(("dp", "mem"), None), P("mem", "dp"), P(("dp", "mem"), None, None)),
        check_vma=False,
    )
```

```python
import functools

import jax
import jax.numpy as jnp
from jax import lax
from jax.experimental import pallas as pl
from jax.experimental.pallas import tpu as pltpu
from jax.sharding import PartitionSpec as P

MESH = pl.DeviceIdType.MESH
X, K, Z, Y = 4, 2, 16, 4
C = X * K
TOK, PICKS, ROWS, FEAT, CAP = 128, 128, 256, 512, 8
HALF = ROWS // 2
SLOTS = Z * CAP
MSG = SLOTS + 16
F32, BF16 = jnp.float32, jnp.bfloat16
NT = (((1,), (1,)), ((), ()))
TN = (((0,), (0,)), ((), ()))


class Ids:
    def __init__(self):
        self.count = 0

    def take(self, number=1):
        first = self.count
        self.count += number
        return first


def exchange(
    slot_t, weight_t, route, og, values,
    out, gv, pair,
    va, oga, wm, wa, ps, dense_t, pm, wt, gt, pt, ip, ir, ic, ix, iy, isrc,
    outp, ytr, ytl, yfr, yfl, rz, sz, ssem, rsem, lsem,
):
    dp, mem = lax.axis_index("dp"), lax.axis_index("mem")
    x, k = dp // K, dp % K
    z, y = mem // Y, mem % Y
    ids = Ids()
    sent = []

    def dev(dx=0, dk=0, dz=0, dy=0):
        to_dp = ((x + dx) % X) * K + (k + dk) % K
        to_mem = ((z + dz) % Z) * Y + (y + dy) % Y
        return (to_dp, to_mem)

    def cof(dx, dk):
        return ((x + dx) % X) * K + (k + dk) % K

    def copy(src, dst, sem, to):
        return pltpu.make_async_remote_copy(
            src_ref=src, dst_ref=dst, send_sem=ssem.at[sem], recv_sem=rsem.at[sem],
            device_id=to, device_id_type=MESH,
        )

    def send(src, dst, sem, to):
        one = copy(src, dst, sem, to)
        one.start()
        sent.append(one)

    def arrived(dst, sem):
        copy(dst, dst, sem, dev(dk=1)).wait_recv()

    def cols(index):
        return pl.ds(pl.multiple_of(index * FEAT, FEAT), FEAT)

    c = dp
    own_v = [
        pltpu.make_async_copy(
            values.at[pl.ds(h * HALF, HALF), cols(c)], va.at[z, h], lsem.at[h]
        )
        for h in range(2)
    ]
    for one in own_v:
        one.start()
    own_og = pltpu.make_async_copy(og.at[:, cols(c)], oga.at[c, y], lsem.at[2])
    own_og.start()

    barrier = pltpu.get_barrier_semaphore()
    others = [(dx, dk) for dx in range(X) for dk in range(K) if (dx, dk) != (0, 0)]
    partners = [dev(dz=1), dev(dz=Z - 1)] + [dev(dy=d) for d in range(1, Y)]
    partners += [dev(dx=dx, dk=dk) for dx, dk in others]
    for partner in partners:
        pl.semaphore_signal(barrier, inc=1, device_id=partner, device_id_type=MESH)
    pl.semaphore_wait(barrier, len(partners))

    hops = {("r", 0): 8, ("l", 0): 7, ("r", 1): 7, ("l", 1): 8}
    zid = {(key, s): ids.take() for key, n in hops.items() for s in range(1, n + 1)}

    def z_send(s, way, h):
        if s <= hops[way, h]:
            if way == "r":
                at, to = (z + Z - s + 1) % Z, dev(dz=1)
            else:
                at, to = (z + s - 1) % Z, dev(dz=Z - 1)
            send(va.at[at, h], va.at[at, h], zid[((way, h), s)], to)

    def z_step(s, h):
        for way in ("r", "l"):
            if s <= hops[way, h]:
                at = (z + Z - s) % Z if way == "r" else (z + s) % Z
                arrived(va.at[at, h], zid[((way, h), s)])
                z_send(s + 1, way, h)

    order = [(0, 0), (0, 1), (1, 0), (1, 1), (3, 0), (3, 1), (2, 0), (2, 1)]
    cid = [ids.take() for _ in order]
    yr1 = [ids.take() for _ in order]
    yl1 = [ids.take() for _ in order]
    y2 = [ids.take() for _ in order]

    def c_send(i):
        dx, dk = order[i]
        to = cof(dx, dk)
        send(og.at[:, cols(to)], oga.at[c, y], cid[i], dev(dx=dx, dk=dk))

    def source(i):
        dx, dk = order[i]
        return cof(X - dx, dk)

    def y_send(i):
        block = oga.at[source(i), y]
        send(block, block, yr1[i], dev(dy=1))
        send(block, block, yl1[i], dev(dy=Y - 1))

    def c_step(i):
        arrived(oga.at[source(i), y], cid[i])
        y_send(i)

    def y_step(i):
        right = oga.at[source(i), (y + Y - 1) % Y]
        left = oga.at[source(i), (y + 1) % Y]
        if i % 2 == 0:
            arrived(right, yr1[i])
            send(right, right, y2[i], dev(dy=1))
            arrived(left, yl1[i])
        else:
            arrived(left, yl1[i])
            send(left, left, y2[i], dev(dy=Y - 1))
            arrived(right, yr1[i])

    def y_last(i):
        arrived(oga.at[source(i), (y + 2) % Y], y2[i])

    w1 = [ids.take() for _ in range(Y)]
    w2 = {(dx, dy): ids.take() for dx in range(X) for dy in range(Y)}
    w3 = {(dx, dy): ids.take() for dx in range(1, X) for dy in range(Y)}

    def w_piece(dy):
        at = (y + Y - dy) % Y
        if dy:
            arrived(wa.at[c, at], w1[dy])
        for dx in (1, 3, 2):
            send(wa.at[c, at], wa.at[c, at], w2[dx, dy], dev(dx=dx))
        send(wa.at[c, at], wa.at[c, at], w2[0, dy], dev(dk=1))

    def w_pass(dx, dy):
        block = wa.at[cof(X - dx, 0), (y + Y - dy) % Y]
        arrived(block, w2[dx, dy])
        send(block, block, w3[dx, dy], dev(dk=1))

    def w_last(dx):
        for dy in range(Y):
            block = wa.at[cof(X - dx, 1), (y + Y - dy) % Y]
            arrived(block, w3[dx, dy] if dx else w2[0, dy])

    for one in own_v:
        one.wait()
    for way, h in hops:
        z_send(1, way, h)
    for i in range(1, 8):
        c_send(i)
    own_og.wait()
    y_send(0)
    c_step(1)

    def dense(a):
        columns = lax.broadcasted_iota(jnp.int32, (128, TOK), 0) + a * 128

        def spread(step, total):
            at = pl.multiple_of(step * 8, 8)
            slot_rows, weight_rows = slot_t[pl.ds(at, 8), :], weight_t[pl.ds(at, 8), :]
            for u in range(8):
                hit = columns == slot_rows[u : u + 1, :]
                total = total + jnp.where(hit, weight_rows[u : u + 1, :], 0.0)
            return total

        total = lax.fori_loop(0, PICKS // 8, spread, jnp.zeros((128, TOK), F32))
        dense_t[pl.ds(a * 128, 128), :] = total.astype(BF16)

    dense(0)
    z_step(1, 0)
    dense(1)
    c_step(2)
    dense(2)
    z_step(1, 1)
    dense(3)

    lane = lax.broadcasted_iota(jnp.int32, (TOK, TOK), 1)
    row = lax.broadcasted_iota(jnp.int32, (TOK, TOK), 0)
    owner = [route[0:1, :], route[1:2, :]]
    number = lax.broadcasted_iota(jnp.int32, (Z * Y, TOK), 0)
    hits = [jnp.where(number == one, 1.0, 0.0) for one in owner]
    earlier = jnp.where(row < lane, 1.0, 0.0).astype(BF16)
    ranks = [jnp.dot(hit.astype(BF16), earlier, preferred_element_type=F32) for hit in hits]
    ranks[1] = ranks[1] + jnp.sum(hits[0], axis=1, keepdims=True)
    ranks = [
        jnp.sum(hit * rank, axis=0, keepdims=True).astype(jnp.int32)
        for hit, rank in zip(hits, ranks)
    ]

    slot_ids = lax.broadcasted_iota(jnp.int32, (SLOTS, TOK), 0)
    for to in range(Y):
        total = jnp.zeros((SLOTS, ROWS), F32)
        lanes = []
        for j in range(2):
            here, group = owner[j] % Y == to, owner[j] // Y
            place = jnp.where(here, group * CAP + ranks[j], -1)
            one = jnp.where(slot_ids == place, 1.0, 0.0).astype(BF16)
            ps[j, pl.ds(to * SLOTS, SLOTS), :] = one
            total = total + lax.dot_general(
                one, dense_t[pl.ds(j * ROWS, ROWS), :], NT, preferred_element_type=F32
            )
            spot = group * (2 * CAP) + ranks[j] + (y % 2) * CAP
            lanes.append(jnp.where(here, spot, -1).astype(F32))
        wm[to, pl.ds(0, SLOTS), :] = total.astype(BF16)
        wm[to, pl.ds(SLOTS, 16), :] = jnp.broadcast_to(
            jnp.concatenate(lanes, axis=1), (16, ROWS)
        ).astype(BF16)
    for dy in (1, 3, 2):
        send(wm.at[(y + dy) % Y], wa.at[c, y], w1[dy], dev(dy=dy))
    wa[c, y] = wm[y]
    w_piece(0)

    c_step(4)
    c_step(3)
    z_step(2, 0)
    c_step(5)
    y_step(0)
    y_step(1)
    z_step(2, 1)
    c_step(6)
    c_step(7)
    w_piece(1)
    w_piece(3)
    z_step(3, 0)
    w_piece(2)
    y_step(2)
    z_step(3, 1)
    y_step(4)
    w_pass(1, 0)
    w_pass(3, 0)
    w_pass(2, 0)
    z_step(4, 0)
    y_step(3)
    w_last(0)
    z_step(4, 1)
    y_step(5)

    def prepare(i):
        src = source(i)

        def half(yp, carry):
            pi = (src % K) * 8 + (src // K) * 2 + yp
            slots = lax.broadcasted_iota(jnp.int32, (ROWS, TOK), 0).astype(F32)
            at = pl.multiple_of(pi * 16, 16)
            parts = []
            for q in range(2):
                row = wa[src, yp * 2 + q, pl.ds(SLOTS, 16), :].astype(F32)[0:1, :]
                hit = jnp.where(slots == row[:, :TOK], 1.0, 0.0)
                hit = hit + jnp.where(slots == row[:, TOK:], 1.0, 0.0)
                pm[pi, :, pl.ds(q * TOK, TOK)] = hit.astype(BF16)
                part = wa[src, yp * 2 + q, pl.ds(0, SLOTS), :].astype(F32)
                parts.append(part.reshape(Z, CAP, ROWS))
            wt[:, pl.ds(at, 16), :] = jnp.concatenate(parts, axis=1).astype(BF16)
            return carry

        lax.fori_loop(0, 2, half, 0)

    def gather(i):
        src = source(i)

        def half(yp, carry):
            pi = (src % K) * 8 + (src // K) * 2 + yp
            at = pl.multiple_of(pi * 16, 16)
            tokens = oga[src, pl.ds(yp * 2, 2)].reshape(2 * TOK, FEAT)
            got = jnp.dot(pm[pi], tokens, preferred_element_type=F32)
            gt[:, pl.ds(at, 16), :] = got.astype(BF16).reshape(Z, 16, FEAT)
            return carry

        lax.fori_loop(0, 2, half, 0)

    def p_step(s):
        def side(u, carry):
            at = (z + Z + (1 - 2 * u) * s) % Z
            rows = va[at].reshape(ROWS, FEAT)
            pt[at] = jnp.dot(wt[at], rows, preferred_element_type=F32).astype(BF16)
            return carry

        lax.fori_loop(0, 1 if s in (0, 8) else 2, side, 0)

    for dy in (1, 3, 2):
        w_pass(1, dy)
        w_pass(3, dy)
    z_step(5, 0)
    for dy in (1, 3, 2):
        w_pass(2, dy)
    prepare(0)
    prepare(1)
    y_step(6)
    y_step(7)
    z_step(5, 1)
    prepare(2)
    prepare(4)
    y_last(0)
    gather(0)
    y_last(1)
    gather(1)
    z_step(6, 0)
    prepare(6)
    w_last(1)
    w_last(3)
    prepare(3)
    prepare(5)
    y_last(2)
    gather(2)
    w_last(2)
    prepare(7)
    z_step(6, 1)
    p_step(0)
    p_step(1)
    y_last(4)
    gather(4)
    p_step(2)
    z_step(7, 0)
    y_last(3)
    gather(3)
    p_step(3)
    p_step(4)
    y_last(5)
    gather(5)
    z_step(7, 1)
    p_step(5)
    p_step(6)
    y_last(6)
    gather(6)
    y_last(7)
    gather(7)

    rid = ids.take(32)

    def grad_part(at, h):
        rows = pl.ds(h * HALF, HALF)
        return lax.dot_general(wt[at, :, rows], gt[at], TN, preferred_element_type=F32)

    def r_step(s, h):
        def stream(way, carry):
            at = (z + Z + (1 - 2 * way) * (8 - s)) % Z
            total = grad_part(at, h)
            if s >= 2:
                arrived(rz.at[s - 1, way, h], rid + (s - 1) * 4 + way * 2 + h)
                total = total + rz[s - 1, way, h].astype(F32)
            sz[s, way, h] = total.astype(BF16)
            if s == 1:

                @pl.when(way == h)
                def _():
                    arrived(rz.at[0, way, h], rid + way * 2 + h)
                    more = total + rz[0, way, h].astype(F32)
                    sz[s, way, h] = more.astype(BF16)

            to_mem = ((z + Z + 1 - 2 * way) % Z) * Y + y
            copy(
                sz.at[s, way, h], rz.at[s, way, h], rid + s * 4 + way * 2 + h, (dp, to_mem)
            ).start()
            return carry

        if s == 0:
            stream(h, 0)
        else:
            lax.fori_loop(0, 2, stream, 0)

    def r_last(h):
        total = grad_part(z, h)
        for way in range(2):
            arrived(rz.at[7, way, h], rid + 28 + way * 2 + h)
            total = total + rz[7, way, h].astype(F32)
        gv[pl.ds(h * HALF, HALF), :] = total

    def r_drain():
        def drain(i, carry):
            block = sz.at[i // 4, (i // 2) % 2, i % 2]

            @pl.when((i != 1) & (i != 2))
            def _():
                copy(block, block, rid + i, dev(dz=1)).wait_send()

            return carry

        lax.fori_loop(0, 32, drain, 0)

    r_step(0, 0)
    r_step(0, 1)
    z_step(8, 0)
    p_step(7)
    z_step(8, 1)
    p_step(8)

    i1 = ids.take()
    i2 = [ids.take() for _ in range(4)]
    i3 = [ids.take() for _ in range(4)]
    m1r = [ids.take() for _ in range(4)]
    m1l = [ids.take() for _ in range(4)]
    mr = [ids.take() for _ in range(8)]
    ml = [ids.take() for _ in range(8)]
    oid = [ids.take() for _ in order]
    far, up, down = (y + 2) % Y, (y + 1) % Y, (y + Y - 1) % Y
    couples = [(6, 7), (2, 3), (4, 5), (0, 1)]

    def to_of(i):
        dx, dk = order[i]
        return cof(dx, dk)

    def scatter(i):
        src = to_of(i)

        def half(yp, carry):
            pi = (src % K) * 8 + (src // K) * 2 + yp
            at = pl.multiple_of(pi * 16, 16)
            parts = pt[:, pl.ds(at, 16), :].reshape(ROWS, FEAT)
            got = lax.dot_general(pm[pi], parts, TN, preferred_element_type=F32)
            outp[src, pl.ds(yp * 2, 2)] = got.astype(BF16).reshape(2, TOK, FEAT)
            return carry

        lax.fori_loop(0, 2, half, 0)

    def m_first(n):
        e, o = couples[n]
        scatter(e)
        send(outp.at[to_of(e), far], ytr.at[n], m1r[n], dev(dy=1))
        send(outp.at[to_of(e), down], yfl.at[e], ml[e], dev(dy=Y - 1))
        scatter(o)
        send(outp.at[to_of(o), far], ytl.at[n], m1l[n], dev(dy=Y - 1))
        send(outp.at[to_of(o), up], yfr.at[o], mr[o], dev(dy=1))

    def m_second(n):
        e, o = couples[n]
        at = to_of(e)
        arrived(ytr.at[n], m1r[n])
        outp[at, up] = (outp[at, up].astype(F32) + ytr[n].astype(F32)).astype(BF16)
        send(outp.at[at, up], yfr.at[e], mr[e], dev(dy=1))
        at = to_of(o)
        arrived(ytl.at[n], m1l[n])
        outp[at, down] = (outp[at, down].astype(F32) + ytl[n].astype(F32)).astype(BF16)
        send(outp.at[at, down], yfl.at[o], ml[o], dev(dy=Y - 1))

    def m_final(n):
        for i in couples[n]:
            dx, dk = order[i]
            to = to_of(i)
            arrived(yfr.at[i], mr[i])
            arrived(yfl.at[i], ml[i])
            total = outp[to, y].astype(F32) + yfr[i].astype(F32) + yfl[i].astype(F32)
            outp[to, y] = total.astype(BF16)
            if i == 0:
                own = pltpu.make_async_copy(outp.at[to, y], out.at[:, cols(c)], lsem.at[3])
                own.start()
                own.wait()
            else:
                send(outp.at[to, y], out.at[:, cols(c)], oid[i], dev(dx=dx, dk=dk))

    def inner(at, carry):
        rows = va[at].reshape(ROWS, FEAT)
        got = lax.dot_general(gt[at], rows, NT, preferred_element_type=F32)
        ip[:, :, at] = got.astype(BF16).reshape(K, X, 32, ROWS)
        return carry

    def add_core(i, carry):
        xx = i // 4
        at = pl.ds((i % 4) * 4, 4)
        ic[xx, at] = (ip[k, xx, at].astype(F32) + ir[xx, at].astype(F32)).astype(BF16)
        return carry

    def add_chips(at, carry):
        total = ic[x, at].astype(F32)
        for i in range(3):
            total = total + ix[i, at].astype(F32)
        for q in range(4):
            iy[q, at] = total[q * CAP : (q + 1) * CAP, :]
        return carry

    m_first(0)
    m_first(1)
    r_step(1, 0)
    m_second(0)
    r_step(1, 1)
    m_first(2)
    lax.fori_loop(0, Z // 2, inner, 0)
    r_step(2, 0)
    m_second(1)
    m_first(3)
    lax.fori_loop(Z // 2, Z, inner, 0)
    send(ip.at[(k + 1) % K], ir, i1, dev(dk=1))
    r_step(2, 1)
    m_final(0)
    r_step(3, 0)
    arrived(ir, i1)
    lax.fori_loop(0, 16, add_core, 0)
    for dx in (1, 3, 2):
        send(ic.at[(x + dx) % X], ix.at[dx - 1], i2[dx], dev(dx=dx))
    r_step(3, 1)
    m_second(2)
    r_step(4, 0)
    m_final(1)
    r_step(4, 1)
    m_second(3)
    r_step(5, 0)
    r_step(5, 1)
    m_final(2)
    for dx in (1, 3, 2):
        arrived(ix.at[dx - 1], i2[dx])
    lax.fori_loop(0, Z, add_chips, 0)
    for q in range(4):
        isrc[4, pl.ds(q * SLOTS, SLOTS), :] = iy[q].reshape(SLOTS, ROWS).astype(BF16)
    isrc[0, pl.ds(0, SLOTS), :] = isrc[4, pl.ds(pl.multiple_of(y * SLOTS, SLOTS), SLOTS), :]
    for i in range(1, 4):
        to = (y + i) % Y
        send(
            isrc.at[4, pl.ds(pl.multiple_of(to * SLOTS, SLOTS), SLOTS), :],
            isrc.at[i, pl.ds(0, SLOTS), :], i3[i], dev(dy=i),
        )
    r_step(6, 0)
    m_final(3)
    r_step(6, 1)
    for i in range(1, 4):
        arrived(isrc.at[i, pl.ds(0, SLOTS), :], i3[i])
    for j in range(2):
        total = jnp.zeros((TOK, ROWS), F32)
        for i in range(4):
            at = pl.multiple_of(((y + Y - i) % Y) * SLOTS, SLOTS)
            total = total + lax.dot_general(
                ps[j, pl.ds(at, SLOTS), :], isrc[i, pl.ds(0, SLOTS), :], TN,
                preferred_element_type=F32,
            )
        pair[:, pl.ds(j * ROWS, ROWS)] = total
    r_step(7, 0)
    r_step(7, 1)
    for i in range(1, 8):
        arrived(out.at[:, cols(source(i))], oid[i])
    r_last(0)
    r_last(1)
    for one in sent:
        one.wait_send()
    r_drain()
    assert ids.count <= SEMS, ids.count


SEMS = 192


def pick(pair_ref, slot_ref, out_in, gv_in, out_ref, out_out, gv_out, sems):
    copies = [
        pltpu.make_async_copy(out_in, out_out, sems.at[0]),
        pltpu.make_async_copy(gv_in, gv_out, sems.at[1]),
    ]
    for one in copies:
        one.start()
    slot = slot_ref[...].T
    low, high = slot & 127, slot // 128
    total = jnp.zeros((TOK, PICKS), F32)
    for a in range(4):
        part = jnp.take_along_axis(pair_ref[:, pl.ds(a * 128, 128)], low, axis=1)
        total = jnp.where(high == a, part, total)
    out_ref[...] = total.T
    for one in copies:
        one.wait()


def shards(lookup_slot, lookup_weight, owner_route, values, out_grad):
    slot_t = lookup_slot.transpose(1, 2, 0).reshape(PICKS, TOK)
    weight_t = lookup_weight.transpose(1, 2, 0).reshape(PICKS, TOK)
    hbm = pl.BlockSpec(memory_space=pltpu.HBM)
    vmem, anywhere = pl.BlockSpec(memory_space=pltpu.VMEM), pl.BlockSpec(memory_space=pl.ANY)
    out, gv, pair = pl.pallas_call(
        exchange,
        out_shape=(
            jax.ShapeDtypeStruct((TOK, C * FEAT), BF16),
            jax.ShapeDtypeStruct((ROWS, FEAT), F32),
            jax.ShapeDtypeStruct((TOK, 2 * ROWS), F32),
        ),
        in_specs=[vmem, vmem, vmem, vmem, anywhere],
        out_specs=(vmem, vmem, vmem),
        scratch_shapes=[
            pltpu.VMEM((Z, 2, HALF, FEAT), BF16),
            pltpu.VMEM((C, Y, TOK, FEAT), BF16),
            pltpu.VMEM((Y, MSG, ROWS), BF16),
            pltpu.VMEM((C, Y, MSG, ROWS), BF16),
            pltpu.VMEM((2, Y * SLOTS, TOK), BF16),
            pltpu.VMEM((2 * ROWS, TOK), BF16),
            pltpu.VMEM((16, ROWS, 2 * TOK), BF16),
            pltpu.VMEM((Z, 16 * 16, ROWS), BF16),
            pltpu.VMEM((Z, 16 * 16, FEAT), BF16),
            pltpu.VMEM((Z, 16 * 16, FEAT), BF16),
            pltpu.VMEM((K, X, Z, 32, ROWS), BF16),
            pltpu.VMEM((X, Z, 32, ROWS), BF16),
            pltpu.VMEM((X, Z, 32, ROWS), BF16),
            pltpu.VMEM((3, Z, 32, ROWS), BF16),
            pltpu.VMEM((4, Z, CAP, ROWS), F32),
            pltpu.VMEM((5, Y * SLOTS, ROWS), BF16),
            pltpu.VMEM((C, Y, TOK, FEAT), BF16),
            pltpu.VMEM((4, TOK, FEAT), BF16),
            pltpu.VMEM((4, TOK, FEAT), BF16),
            pltpu.VMEM((C, TOK, FEAT), BF16),
            pltpu.VMEM((C, TOK, FEAT), BF16),
            pltpu.VMEM((8, 2, 2, HALF, FEAT), BF16),
            pltpu.VMEM((8, 2, 2, HALF, FEAT), BF16),
            pltpu.SemaphoreType.DMA((SEMS,)),
            pltpu.SemaphoreType.DMA((SEMS,)),
            pltpu.SemaphoreType.DMA((4,)),
        ],
        compiler_params=pltpu.CompilerParams(
            collective_id=0, has_side_effects=True, vmem_limit_bytes=58 * 1024 * 1024
        ),
        name="exchange",
    )(slot_t, weight_t, owner_route.T, out_grad, values)
    grad_weight, out, gv = pl.pallas_call(
        pick,
        out_shape=(
            jax.ShapeDtypeStruct((PICKS, TOK), F32),
            jax.ShapeDtypeStruct(out.shape, out.dtype),
            jax.ShapeDtypeStruct(gv.shape, gv.dtype),
        ),
        in_specs=[vmem, vmem, vmem, vmem],
        out_specs=(vmem, hbm, hbm),
        scratch_shapes=[pltpu.SemaphoreType.DMA((2,))],
        name="pick",
    )(pair, slot_t, out, gv)
    return out, gv, grad_weight.reshape(4, 32, TOK).transpose(2, 0, 1)


def solution(mesh):
    return jax.shard_map(
        shards,
        mesh=mesh,
        in_specs=(
            P(("dp", "mem"), None, None),
            P(("dp", "mem"), None, None),
            P(("dp", "mem"), None),
            P("mem", None),
            P(("dp", "mem"), None),
        ),
        out_specs=(P(("dp", "mem"), None), P("mem", "dp"), P(("dp", "mem"), None, None)),
        check_vma=False,
    )
```

```python
import functools

import jax
import jax.numpy as jnp
from jax import lax
from jax.experimental import pallas as pl
from jax.experimental.pallas import tpu as pltpu
from jax.sharding import PartitionSpec as P

MESH = pl.DeviceIdType.MESH
X, K, Z, Y = 4, 2, 16, 4
C = X * K
TOK, PICKS, ROWS, FEAT, CAP = 128, 128, 256, 512, 8
HALF = ROWS // 2
SLOTS = Z * CAP
MSG = SLOTS + 16
F32, BF16 = jnp.float32, jnp.bfloat16
NT = (((1,), (1,)), ((), ()))
TN = (((0,), (0,)), ((), ()))


class Ids:
    def __init__(self):
        self.count = 0

    def take(self, number=1):
        first = self.count
        self.count += number
        return first


def exchange(
    slot_in, weight_in, route_in, og, values,
    out, gv, pair,
    va, oga, wm, wa, ps, dense_t, slot_t, weight_t, route, pair_v, pm, wt, gt, pt, ip, ir, ic, ix, iy, isrc,
    outp, ytr, ytl, yfr, yfl, rz, sz, ssem, rsem, lsem,
):
    dp, mem = lax.axis_index("dp"), lax.axis_index("mem")
    x, k = dp // K, dp % K
    z, y = mem // Y, mem % Y
    ids = Ids()
    sent = []

    def dev(dx=0, dk=0, dz=0, dy=0):
        to_dp = ((x + dx) % X) * K + (k + dk) % K
        to_mem = ((z + dz) % Z) * Y + (y + dy) % Y
        return (to_dp, to_mem)

    def cof(dx, dk):
        return ((x + dx) % X) * K + (k + dk) % K

    def copy(src, dst, sem, to):
        return pltpu.make_async_remote_copy(
            src_ref=src, dst_ref=dst, send_sem=ssem.at[sem], recv_sem=rsem.at[sem],
            device_id=to, device_id_type=MESH,
        )

    def send(src, dst, sem, to):
        one = copy(src, dst, sem, to)
        one.start()
        sent.append(one)

    def arrived(dst, sem):
        copy(dst, dst, sem, dev(dk=1)).wait_recv()

    def cols(index):
        return pl.ds(pl.multiple_of(index * FEAT, FEAT), FEAT)

    c = dp
    own_v = [
        pltpu.make_async_copy(
            values.at[pl.ds(h * HALF, HALF), cols(c)], va.at[z, h], lsem.at[h]
        )
        for h in range(2)
    ]
    for one in own_v:
        one.start()
    own_og = pltpu.make_async_copy(og.at[:, cols(c)], oga.at[c, y], lsem.at[2])
    own_og.start()
    tables = [
        pltpu.make_async_copy(slot_in, slot_t, lsem.at[4]),
        pltpu.make_async_copy(weight_in, weight_t, lsem.at[5]),
        pltpu.make_async_copy(route_in, route, lsem.at[7]),
    ]
    for one in tables:
        one.start()

    barrier = pltpu.get_barrier_semaphore()
    others = [(dx, dk) for dx in range(X) for dk in range(K) if (dx, dk) != (0, 0)]
    partners = [dev(dz=1), dev(dz=Z - 1)] + [dev(dy=d) for d in range(1, Y)]
    partners += [dev(dx=dx, dk=dk) for dx, dk in others]
    for partner in partners:
        pl.semaphore_signal(barrier, inc=1, device_id=partner, device_id_type=MESH)
    pl.semaphore_wait(barrier, len(partners))

    hops = {("r", 0): 8, ("l", 0): 7, ("r", 1): 7, ("l", 1): 8}
    zid = {(key, s): ids.take() for key, n in hops.items() for s in range(1, n + 1)}

    def z_send(s, way, h):
        if s <= hops[way, h]:
            if way == "r":
                at, to = (z + Z - s + 1) % Z, dev(dz=1)
            else:
                at, to = (z + s - 1) % Z, dev(dz=Z - 1)
            send(va.at[at, h], va.at[at, h], zid[((way, h), s)], to)

    def z_step(s, h):
        for way in ("r", "l"):
            if s <= hops[way, h]:
                at = (z + Z - s) % Z if way == "r" else (z + s) % Z
                arrived(va.at[at, h], zid[((way, h), s)])
                z_send(s + 1, way, h)

    order = [(0, 0), (0, 1), (1, 0), (1, 1), (3, 0), (3, 1), (2, 0), (2, 1)]
    cid = [ids.take() for _ in order]
    yr1 = [ids.take() for _ in order]
    yl1 = [ids.take() for _ in order]
    y2 = [ids.take() for _ in order]

    def c_send(i):
        dx, dk = order[i]
        to = cof(dx, dk)
        send(og.at[:, cols(to)], oga.at[c, y], cid[i], dev(dx=dx, dk=dk))

    def source(i):
        dx, dk = order[i]
        return cof(X - dx, dk)

    def y_send(i):
        block = oga.at[source(i), y]
        send(block, block, yr1[i], dev(dy=1))
        send(block, block, yl1[i], dev(dy=Y - 1))

    def c_step(i):
        arrived(oga.at[source(i), y], cid[i])
        y_send(i)

    def y_step(i):
        right = oga.at[source(i), (y + Y - 1) % Y]
        left = oga.at[source(i), (y + 1) % Y]
        if i % 2 == 0:
            arrived(right, yr1[i])
            send(right, right, y2[i], dev(dy=1))
            arrived(left, yl1[i])
        else:
            arrived(left, yl1[i])
            send(left, left, y2[i], dev(dy=Y - 1))
            arrived(right, yr1[i])

    def y_last(i):
        arrived(oga.at[source(i), (y + 2) % Y], y2[i])

    w1 = [ids.take() for _ in range(Y)]
    w2 = {(dx, dy): ids.take() for dx in range(X) for dy in range(Y)}
    w3 = {(dx, dy): ids.take() for dx in range(1, X) for dy in range(Y)}

    def w_piece(dy):
        at = (y + Y - dy) % Y
        if dy:
            arrived(wa.at[c, at], w1[dy])
        for dx in (1, 3, 2):
            send(wa.at[c, at], wa.at[c, at], w2[dx, dy], dev(dx=dx))
        send(wa.at[c, at], wa.at[c, at], w2[0, dy], dev(dk=1))

    def w_pass(dx, dy):
        block = wa.at[cof(X - dx, 0), (y + Y - dy) % Y]
        arrived(block, w2[dx, dy])
        send(block, block, w3[dx, dy], dev(dk=1))

    def w_last(dx):
        for dy in range(Y):
            block = wa.at[cof(X - dx, 1), (y + Y - dy) % Y]
            arrived(block, w3[dx, dy] if dx else w2[0, dy])

    for one in own_v:
        one.wait()
    for way, h in hops:
        z_send(1, way, h)
    for i in range(1, 8):
        c_send(i)
    own_og.wait()
    y_send(0)
    c_step(1)

    def dense(a):
        columns = lax.broadcasted_iota(jnp.int32, (128, TOK), 0) + a * 128

        def spread(step, total):
            at = pl.multiple_of(step * 8, 8)
            slot_rows, weight_rows = slot_t[pl.ds(at, 8), :], weight_t[pl.ds(at, 8), :]
            for u in range(8):
                hit = columns == slot_rows[u : u + 1, :]
                total = total + jnp.where(hit, weight_rows[u : u + 1, :], 0.0)
            return total

        total = lax.fori_loop(0, PICKS // 8, spread, jnp.zeros((128, TOK), F32))
        dense_t[pl.ds(a * 128, 128), :] = total.astype(BF16)

    for one in tables:
        one.wait()
    dense(0)
    z_step(1, 0)
    dense(1)
    c_step(2)
    dense(2)
    z_step(1, 1)
    dense(3)

    lane = lax.broadcasted_iota(jnp.int32, (TOK, TOK), 1)
    row = lax.broadcasted_iota(jnp.int32, (TOK, TOK), 0)
    owner = [route[0:1, :], route[1:2, :]]
    number = lax.broadcasted_iota(jnp.int32, (Z * Y, TOK), 0)
    hits = [jnp.where(number == one, 1.0, 0.0) for one in owner]
    earlier = jnp.where(row < lane, 1.0, 0.0).astype(BF16)
    ranks = [jnp.dot(hit.astype(BF16), earlier, preferred_element_type=F32) for hit in hits]
    ranks[1] = ranks[1] + jnp.sum(hits[0], axis=1, keepdims=True)
    ranks = [
        jnp.sum(hit * rank, axis=0, keepdims=True).astype(jnp.int32)
        for hit, rank in zip(hits, ranks)
    ]

    slot_ids = lax.broadcasted_iota(jnp.int32, (SLOTS, TOK), 0)
    for to in range(Y):
        total = jnp.zeros((SLOTS, ROWS), F32)
        lanes = []
        for j in range(2):
            here, group = owner[j] % Y == to, owner[j] // Y
            place = jnp.where(here, group * CAP + ranks[j], -1)
            one = jnp.where(slot_ids == place, 1.0, 0.0).astype(BF16)
            ps[j, pl.ds(to * SLOTS, SLOTS), :] = one
            total = total + lax.dot_general(
                one, dense_t[pl.ds(j * ROWS, ROWS), :], NT, preferred_element_type=F32
            )
            spot = group * (2 * CAP) + ranks[j] + (y % 2) * CAP
            lanes.append(jnp.where(here, spot, -1).astype(F32))
        wm[to, pl.ds(0, SLOTS), :] = total.astype(BF16)
        wm[to, pl.ds(SLOTS, 16), :] = jnp.broadcast_to(
            jnp.concatenate(lanes, axis=1), (16, ROWS)
        ).astype(BF16)
    for dy in (1, 3, 2):
        send(wm.at[(y + dy) % Y], wa.at[c, y], w1[dy], dev(dy=dy))
    wa[c, y] = wm[y]
    w_piece(0)

    c_step(4)
    c_step(3)
    z_step(2, 0)
    c_step(5)
    y_step(0)
    y_step(1)
    z_step(2, 1)
    c_step(6)
    c_step(7)
    w_piece(1)
    w_piece(3)
    z_step(3, 0)
    w_piece(2)
    y_step(2)
    z_step(3, 1)
    y_step(4)
    w_pass(1, 0)
    w_pass(3, 0)
    w_pass(2, 0)
    z_step(4, 0)
    y_step(3)
    w_last(0)
    z_step(4, 1)
    y_step(5)

    def prepare(i):
        src = source(i)

        def half(yp, carry):
            pi = (src % K) * 8 + (src // K) * 2 + yp
            slots = lax.broadcasted_iota(jnp.int32, (ROWS, TOK), 0).astype(F32)
            at = pl.multiple_of(pi * 16, 16)
            parts = []
            for q in range(2):
                row = wa[src, yp * 2 + q, pl.ds(SLOTS, 16), :].astype(F32)[0:1, :]
                hit = jnp.where(slots == row[:, :TOK], 1.0, 0.0)
                hit = hit + jnp.where(slots == row[:, TOK:], 1.0, 0.0)
                pm[pi, :, pl.ds(q * TOK, TOK)] = hit.astype(BF16)
                part = wa[src, yp * 2 + q, pl.ds(0, SLOTS), :].astype(F32)
                parts.append(part.reshape(Z, CAP, ROWS))
            wt[:, pl.ds(at, 16), :] = jnp.concatenate(parts, axis=1).astype(BF16)
            return carry

        lax.fori_loop(0, 2, half, 0)

    def gather(i):
        src = source(i)

        def half(yp, carry):
            pi = (src % K) * 8 + (src // K) * 2 + yp
            at = pl.multiple_of(pi * 16, 16)
            tokens = oga[src, pl.ds(yp * 2, 2)].reshape(2 * TOK, FEAT)
            got = jnp.dot(pm[pi], tokens, preferred_element_type=F32)
            gt[:, pl.ds(at, 16), :] = got.astype(BF16).reshape(Z, 16, FEAT)
            return carry

        lax.fori_loop(0, 2, half, 0)

    def p_step(s):
        def side(u, carry):
            at = (z + Z + (1 - 2 * u) * s) % Z
            rows = va[at].reshape(ROWS, FEAT)
            pt[at] = jnp.dot(wt[at], rows, preferred_element_type=F32).astype(BF16)
            return carry

        lax.fori_loop(0, 1 if s in (0, 8) else 2, side, 0)

    rid = ids.take(32)

    def grad_part(at, h):
        rows = pl.ds(h * HALF, HALF)
        return lax.dot_general(wt[at, :, rows], gt[at], TN, preferred_element_type=F32)

    def r_step(s, h):
        def stream(way, carry):
            at = (z + Z + (1 - 2 * way) * (8 - s)) % Z
            total = grad_part(at, h)
            if s >= 2:
                arrived(rz.at[s - 1, way, h], rid + (s - 1) * 4 + way * 2 + h)
                total = total + rz[s - 1, way, h].astype(F32)
            sz[s, way, h] = total.astype(BF16)
            if s == 1:

                @pl.when(way == h)
                def _():
                    arrived(rz.at[0, way, h], rid + way * 2 + h)
                    more = total + rz[0, way, h].astype(F32)
                    sz[s, way, h] = more.astype(BF16)

            to_mem = ((z + Z + 1 - 2 * way) % Z) * Y + y
            copy(
                sz.at[s, way, h], rz.at[s, way, h], rid + s * 4 + way * 2 + h, (dp, to_mem)
            ).start()
            return carry

        if s == 0:
            stream(h, 0)
        else:
            lax.fori_loop(0, 2, stream, 0)

    def r_last(h):
        total = grad_part(z, h)
        for way in range(2):
            arrived(rz.at[7, way, h], rid + 28 + way * 2 + h)
            total = total + rz[7, way, h].astype(F32)
        gv[pl.ds(h * HALF, HALF), :] = total

    def r_drain():
        def drain(i, carry):
            block = sz.at[i // 4, (i // 2) % 2, i % 2]

            @pl.when((i != 1) & (i != 2))
            def _():
                copy(block, block, rid + i, dev(dz=1)).wait_send()

            return carry

        lax.fori_loop(0, 32, drain, 0)

    i1 = ids.take()
    i2 = [ids.take() for _ in range(4)]
    i3 = [ids.take() for _ in range(4)]
    m1r = [ids.take() for _ in range(4)]
    m1l = [ids.take() for _ in range(4)]
    mr = [ids.take() for _ in range(8)]
    ml = [ids.take() for _ in range(8)]
    oid = [ids.take() for _ in order]
    far, up, down = (y + 2) % Y, (y + 1) % Y, (y + Y - 1) % Y
    couples = [(6, 7), (2, 3), (4, 5), (0, 1)]

    def to_of(i):
        dx, dk = order[i]
        return cof(dx, dk)

    def scatter(i):
        src = to_of(i)

        def half(yp, carry):
            pi = (src % K) * 8 + (src // K) * 2 + yp
            at = pl.multiple_of(pi * 16, 16)
            parts = pt[:, pl.ds(at, 16), :].reshape(ROWS, FEAT)
            got = lax.dot_general(pm[pi], parts, TN, preferred_element_type=F32)
            outp[src, pl.ds(yp * 2, 2)] = got.astype(BF16).reshape(2, TOK, FEAT)
            return carry

        lax.fori_loop(0, 2, half, 0)

    def m_first(n):
        e, o = couples[n]
        scatter(e)
        send(outp.at[to_of(e), far], ytr.at[n], m1r[n], dev(dy=1))
        send(outp.at[to_of(e), down], yfl.at[e], ml[e], dev(dy=Y - 1))
        scatter(o)
        send(outp.at[to_of(o), far], ytl.at[n], m1l[n], dev(dy=Y - 1))
        send(outp.at[to_of(o), up], yfr.at[o], mr[o], dev(dy=1))

    def m_second(n):
        e, o = couples[n]
        at = to_of(e)
        arrived(ytr.at[n], m1r[n])
        outp[at, up] = (outp[at, up].astype(F32) + ytr[n].astype(F32)).astype(BF16)
        send(outp.at[at, up], yfr.at[e], mr[e], dev(dy=1))
        at = to_of(o)
        arrived(ytl.at[n], m1l[n])
        outp[at, down] = (outp[at, down].astype(F32) + ytl[n].astype(F32)).astype(BF16)
        send(outp.at[at, down], yfl.at[o], ml[o], dev(dy=Y - 1))

    def m_final(n):
        for i in couples[n]:
            dx, dk = order[i]
            to = to_of(i)
            arrived(yfr.at[i], mr[i])
            arrived(yfl.at[i], ml[i])
            total = outp[to, y].astype(F32) + yfr[i].astype(F32) + yfl[i].astype(F32)
            outp[to, y] = total.astype(BF16)
            if i == 0:
                own = pltpu.make_async_copy(outp.at[to, y], out.at[:, cols(c)], lsem.at[3])
                own.start()
                own.wait()
            else:
                send(outp.at[to, y], out.at[:, cols(c)], oid[i], dev(dx=dx, dk=dk))

    def inner(at, carry):
        rows = va[at].reshape(ROWS, FEAT)
        got = lax.dot_general(gt[at], rows, NT, preferred_element_type=F32)
        ip[:, :, at] = got.astype(BF16).reshape(K, X, 32, ROWS)
        return carry

    def add_core(i, carry):
        xx = i // 4
        at = pl.ds((i % 4) * 4, 4)
        ic[xx, at] = (ip[k, xx, at].astype(F32) + ir[xx, at].astype(F32)).astype(BF16)
        return carry

    def add_chips(at, carry):
        total = ic[x, at].astype(F32)
        for i in range(3):
            total = total + ix[i, at].astype(F32)
        for q in range(4):
            iy[q, at] = total[q * CAP : (q + 1) * CAP, :]
        return carry

    for dy in (1, 3, 2):
        w_pass(1, dy)
        w_pass(3, dy)
    z_step(5, 0)
    for dy in (1, 3, 2):
        w_pass(2, dy)
    prepare(0)
    prepare(1)
    y_step(6)
    y_step(7)
    z_step(5, 1)
    prepare(2)
    prepare(4)
    y_last(0)
    gather(0)
    y_last(1)
    gather(1)
    z_step(6, 0)
    prepare(6)
    w_last(1)
    w_last(3)
    prepare(3)
    prepare(5)
    y_last(2)
    gather(2)
    w_last(2)
    prepare(7)
    z_step(6, 1)
    for step in range(4):
        p_step(step)
    y_last(3)
    gather(3)
    y_last(4)
    gather(4)
    z_step(7, 0)
    p_step(4)
    p_step(5)
    y_last(5)
    gather(5)
    for i in (6, 7):
        y_last(i)
        gather(i)
    r_step(0, 0)
    z_step(7, 1)
    r_step(0, 1)
    p_step(6)
    z_step(8, 0)
    p_step(7)
    z_step(8, 1)
    p_step(8)
    m_first(0)
    m_first(1)
    r_step(1, 0)
    r_step(1, 1)
    lax.fori_loop(0, Z // 2, inner, 0)
    r_step(2, 0)
    m_second(0)
    m_first(2)
    r_step(2, 1)
    lax.fori_loop(Z // 2, Z, inner, 0)
    send(ip.at[(k + 1) % K], ir, i1, dev(dk=1))
    r_step(3, 0)
    m_second(1)
    m_first(3)
    r_step(3, 1)
    arrived(ir, i1)
    lax.fori_loop(0, 16, add_core, 0)
    for dx in (1, 3, 2):
        send(ic.at[(x + dx) % X], ix.at[dx - 1], i2[dx], dev(dx=dx))
    r_step(4, 0)
    m_final(0)
    r_step(4, 1)
    m_second(2)
    r_step(5, 0)
    r_step(5, 1)
    m_final(1)
    r_step(6, 0)
    m_second(3)
    for dx in (1, 3, 2):
        arrived(ix.at[dx - 1], i2[dx])
    lax.fori_loop(0, Z, add_chips, 0)
    for q in range(4):
        isrc[4, pl.ds(q * SLOTS, SLOTS), :] = iy[q].reshape(SLOTS, ROWS).astype(BF16)
    isrc[0, pl.ds(0, SLOTS), :] = isrc[4, pl.ds(pl.multiple_of(y * SLOTS, SLOTS), SLOTS), :]
    for i in range(1, 4):
        to = (y + i) % Y
        send(
            isrc.at[4, pl.ds(pl.multiple_of(to * SLOTS, SLOTS), SLOTS), :],
            isrc.at[i, pl.ds(0, SLOTS), :], i3[i], dev(dy=i),
        )
    r_step(6, 1)
    r_step(7, 0)
    m_final(2)
    r_step(7, 1)
    for i in range(1, 4):
        arrived(isrc.at[i, pl.ds(0, SLOTS), :], i3[i])
    for j in range(2):
        total = jnp.zeros((TOK, ROWS), F32)
        for i in range(4):
            at = pl.multiple_of(((y + Y - i) % Y) * SLOTS, SLOTS)
            total = total + lax.dot_general(
                ps[j, pl.ds(at, SLOTS), :], isrc[i, pl.ds(0, SLOTS), :], TN,
                preferred_element_type=F32,
            )
        pair_v[:, pl.ds(j * ROWS, ROWS)] = total
    pair_out = pltpu.make_async_copy(pair_v, pair, lsem.at[6])
    pair_out.start()
    m_final(3)
    r_last(0)
    for i in range(1, 8):
        arrived(out.at[:, cols(source(i))], oid[i])
    r_last(1)
    pair_out.wait()
    for one in sent:
        one.wait_send()
    r_drain()
    assert ids.count <= SEMS, ids.count


SEMS = 192


def pick(pair_ref, slot_ref, out_in, gv_in, out_ref, out_out, gv_out, out_v, gv_v, sems):
    rows = TOK // 2
    parts = [pl.ds(0, rows), pl.ds(rows, rows)]
    fetch = [
        pltpu.make_async_copy(out_in.at[part], out_v.at[part], sems.at[n])
        for n, part in enumerate(parts)
    ]
    fetch.append(pltpu.make_async_copy(gv_in, gv_v, sems.at[2]))
    put = [
        pltpu.make_async_copy(out_v.at[part], out_out.at[part], sems.at[3 + n])
        for n, part in enumerate(parts)
    ]
    put.append(pltpu.make_async_copy(gv_v, gv_out, sems.at[5]))
    for one in fetch:
        one.start()
    slot = slot_ref[...].T
    low, high = slot & 127, slot // 128
    for one, two in zip(fetch, put):
        one.wait()
        two.start()
    total = jnp.zeros((TOK, PICKS), F32)
    for a in range(4):
        part = jnp.take_along_axis(pair_ref[:, pl.ds(a * 128, 128)], low, axis=1)
        total = jnp.where(high == a, part, total)
    out_ref[...] = total.T
    for one in put:
        one.wait()


def shards(lookup_slot, lookup_weight, owner_route, values, out_grad):
    slot_t = lookup_slot.transpose(1, 2, 0).reshape(PICKS, TOK)
    weight_t = lookup_weight.transpose(1, 2, 0).reshape(PICKS, TOK)
    hbm = pl.BlockSpec(memory_space=pltpu.HBM)
    vmem, anywhere = pl.BlockSpec(memory_space=pltpu.VMEM), pl.BlockSpec(memory_space=pl.ANY)
    out, gv, pair = pl.pallas_call(
        exchange,
        out_shape=(
            jax.ShapeDtypeStruct((TOK, C * FEAT), BF16),
            jax.ShapeDtypeStruct((ROWS, FEAT), F32),
            jax.ShapeDtypeStruct((TOK, 2 * ROWS), F32),
        ),
        in_specs=[anywhere] * 5,
        out_specs=(anywhere, vmem, anywhere),
        scratch_shapes=[
            pltpu.VMEM((Z, 2, HALF, FEAT), BF16),
            pltpu.VMEM((C, Y, TOK, FEAT), BF16),
            pltpu.VMEM((Y, MSG, ROWS), BF16),
            pltpu.VMEM((C, Y, MSG, ROWS), BF16),
            pltpu.VMEM((2, Y * SLOTS, TOK), BF16),
            pltpu.VMEM((2 * ROWS, TOK), BF16),
            pltpu.VMEM((PICKS, TOK), jnp.int32),
            pltpu.VMEM((PICKS, TOK), F32),
            pltpu.VMEM((2, TOK), jnp.int32),
            pltpu.VMEM((TOK, 2 * ROWS), F32),
            pltpu.VMEM((16, ROWS, 2 * TOK), BF16),
            pltpu.VMEM((Z, 16 * 16, ROWS), BF16),
            pltpu.VMEM((Z, 16 * 16, FEAT), BF16),
            pltpu.VMEM((Z, 16 * 16, FEAT), BF16),
            pltpu.VMEM((K, X, Z, 32, ROWS), BF16),
            pltpu.VMEM((X, Z, 32, ROWS), BF16),
            pltpu.VMEM((X, Z, 32, ROWS), BF16),
            pltpu.VMEM((3, Z, 32, ROWS), BF16),
            pltpu.VMEM((4, Z, CAP, ROWS), F32),
            pltpu.VMEM((5, Y * SLOTS, ROWS), BF16),
            pltpu.VMEM((C, Y, TOK, FEAT), BF16),
            pltpu.VMEM((4, TOK, FEAT), BF16),
            pltpu.VMEM((4, TOK, FEAT), BF16),
            pltpu.VMEM((C, TOK, FEAT), BF16),
            pltpu.VMEM((C, TOK, FEAT), BF16),
            pltpu.VMEM((8, 2, 2, HALF, FEAT), BF16),
            pltpu.VMEM((8, 2, 2, HALF, FEAT), BF16),
            pltpu.SemaphoreType.DMA((SEMS,)),
            pltpu.SemaphoreType.DMA((SEMS,)),
            pltpu.SemaphoreType.DMA((8,)),
        ],
        compiler_params=pltpu.CompilerParams(
            collective_id=0, has_side_effects=True, vmem_limit_bytes=58 * 1024 * 1024
        ),
        name="exchange",
    )(slot_t, weight_t, owner_route.T, out_grad, values)
    grad_weight, out, gv = pl.pallas_call(
        pick,
        out_shape=(
            jax.ShapeDtypeStruct((PICKS, TOK), F32),
            jax.ShapeDtypeStruct(out.shape, out.dtype),
            jax.ShapeDtypeStruct(gv.shape, gv.dtype),
        ),
        in_specs=[vmem, vmem, hbm, hbm],
        out_specs=(vmem, hbm, hbm),
        scratch_shapes=[
            pltpu.VMEM((TOK, C * FEAT), BF16),
            pltpu.VMEM((ROWS, FEAT), F32),
            pltpu.SemaphoreType.DMA((6,)),
        ],
        name="pick",
    )(pair, slot_t, out, gv)
    return out, gv, grad_weight.reshape(4, 32, TOK).transpose(2, 0, 1)


def solution(mesh):
    return jax.shard_map(
        shards,
        mesh=mesh,
        in_specs=(
            P(("dp", "mem"), None, None),
            P(("dp", "mem"), None, None),
            P(("dp", "mem"), None),
            P("mem", None),
            P(("dp", "mem"), None),
        ),
        out_specs=(P(("dp", "mem"), None), P("mem", "dp"), P(("dp", "mem"), None, None)),
        check_vma=False,
    )
```

```python
import functools

import jax
import jax.numpy as jnp
from jax import lax
from jax.experimental import pallas as pl
from jax.experimental.pallas import tpu as pltpu
from jax.sharding import PartitionSpec as P

MESH = pl.DeviceIdType.MESH
X, K, Z, Y = 4, 2, 16, 4
C = X * K
TOK, PICKS, ROWS, FEAT, CAP = 128, 128, 256, 512, 8
HALF = ROWS // 2
SLOTS = Z * CAP
MSG = SLOTS + 16
F32, BF16 = jnp.float32, jnp.bfloat16
NT = (((1,), (1,)), ((), ()))
TN = (((0,), (0,)), ((), ()))


class Ids:
    def __init__(self):
        self.count = 0

    def take(self, number=1):
        first = self.count
        self.count += number
        return first


def exchange(
    slot_in, weight_in, route_in, og, values,
    out, gv, pair,
    va, oga, wm, wa, ps, dense_t, slot_t, weight_t, route, pair_v, gv_v, pm, wt, gt, pt, ip, ir, ic, ix, iy, isrc,
    outp, ytr, ytl, yfr, yfl, rz, sz, ssem, rsem, lsem,
):
    dp, mem = lax.axis_index("dp"), lax.axis_index("mem")
    x, k = dp // K, dp % K
    z, y = mem // Y, mem % Y
    ids = Ids()
    sent = []

    def dev(dx=0, dk=0, dz=0, dy=0):
        to_dp = ((x + dx) % X) * K + (k + dk) % K
        to_mem = ((z + dz) % Z) * Y + (y + dy) % Y
        return (to_dp, to_mem)

    def cof(dx, dk):
        return ((x + dx) % X) * K + (k + dk) % K

    def copy(src, dst, sem, to):
        return pltpu.make_async_remote_copy(
            src_ref=src, dst_ref=dst, send_sem=ssem.at[sem], recv_sem=rsem.at[sem],
            device_id=to, device_id_type=MESH,
        )

    def send(src, dst, sem, to):
        one = copy(src, dst, sem, to)
        one.start()
        sent.append(one)

    def arrived(dst, sem):
        copy(dst, dst, sem, dev(dk=1)).wait_recv()

    def cols(index):
        return pl.ds(pl.multiple_of(index * FEAT, FEAT), FEAT)

    c = dp
    own_v = [
        pltpu.make_async_copy(
            values.at[pl.ds(h * HALF, HALF), cols(c)], va.at[z, h], lsem.at[h]
        )
        for h in range(2)
    ]
    for one in own_v:
        one.start()
    own_og = pltpu.make_async_copy(og.at[:, cols(c)], oga.at[c, y], lsem.at[2])
    own_og.start()
    tables = [
        pltpu.make_async_copy(slot_in, slot_t, lsem.at[4]),
        pltpu.make_async_copy(weight_in, weight_t, lsem.at[5]),
        pltpu.make_async_copy(route_in, route, lsem.at[7]),
    ]
    for one in tables:
        one.start()

    barrier = pltpu.get_barrier_semaphore()
    others = [(dx, dk) for dx in range(X) for dk in range(K) if (dx, dk) != (0, 0)]
    partners = [dev(dz=1), dev(dz=Z - 1)] + [dev(dy=d) for d in range(1, Y)]
    partners += [dev(dx=dx, dk=dk) for dx, dk in others]
    for partner in partners:
        pl.semaphore_signal(barrier, inc=1, device_id=partner, device_id_type=MESH)
    pl.semaphore_wait(barrier, len(partners))

    hops = {("r", 0): 8, ("l", 0): 7, ("r", 1): 7, ("l", 1): 8}
    zid = {(key, s): ids.take() for key, n in hops.items() for s in range(1, n + 1)}

    def z_send(s, way, h):
        if s <= hops[way, h]:
            if way == "r":
                at, to = (z + Z - s + 1) % Z, dev(dz=1)
            else:
                at, to = (z + s - 1) % Z, dev(dz=Z - 1)
            send(va.at[at, h], va.at[at, h], zid[((way, h), s)], to)

    def z_step(s, h):
        for way in ("r", "l"):
            if s <= hops[way, h]:
                at = (z + Z - s) % Z if way == "r" else (z + s) % Z
                arrived(va.at[at, h], zid[((way, h), s)])
                z_send(s + 1, way, h)

    order = [(0, 0), (0, 1), (1, 0), (1, 1), (3, 0), (3, 1), (2, 0), (2, 1)]
    cid = [ids.take() for _ in order]
    yr1 = [ids.take() for _ in order]
    yl1 = [ids.take() for _ in order]
    y2 = [ids.take() for _ in order]

    def c_send(i):
        dx, dk = order[i]
        to = cof(dx, dk)
        send(og.at[:, cols(to)], oga.at[c, y], cid[i], dev(dx=dx, dk=dk))

    def source(i):
        dx, dk = order[i]
        return cof(X - dx, dk)

    def y_send(i):
        block = oga.at[source(i), y]
        send(block, block, yr1[i], dev(dy=1))
        send(block, block, yl1[i], dev(dy=Y - 1))

    def c_step(i):
        arrived(oga.at[source(i), y], cid[i])
        y_send(i)

    def y_step(i):
        right = oga.at[source(i), (y + Y - 1) % Y]
        left = oga.at[source(i), (y + 1) % Y]
        if i % 2 == 0:
            arrived(right, yr1[i])
            send(right, right, y2[i], dev(dy=1))
            arrived(left, yl1[i])
        else:
            arrived(left, yl1[i])
            send(left, left, y2[i], dev(dy=Y - 1))
            arrived(right, yr1[i])

    def y_last(i):
        arrived(oga.at[source(i), (y + 2) % Y], y2[i])

    w1 = [ids.take() for _ in range(Y)]
    w2 = {(dx, dy): ids.take() for dx in range(X) for dy in range(Y)}
    w3 = {(dx, dy): ids.take() for dx in range(1, X) for dy in range(Y)}

    def w_piece(dy):
        at = (y + Y - dy) % Y
        if dy:
            arrived(wa.at[c, at], w1[dy])
        for dx in (1, 3, 2):
            send(wa.at[c, at], wa.at[c, at], w2[dx, dy], dev(dx=dx))
        send(wa.at[c, at], wa.at[c, at], w2[0, dy], dev(dk=1))

    def w_pass(dx, dy):
        block = wa.at[cof(X - dx, 0), (y + Y - dy) % Y]
        arrived(block, w2[dx, dy])
        send(block, block, w3[dx, dy], dev(dk=1))

    def w_last(dx):
        for dy in range(Y):
            block = wa.at[cof(X - dx, 1), (y + Y - dy) % Y]
            arrived(block, w3[dx, dy] if dx else w2[0, dy])

    for one in own_v:
        one.wait()
    for way, h in hops:
        z_send(1, way, h)
    for i in range(1, 8):
        c_send(i)
    own_og.wait()
    y_send(0)
    c_step(1)

    def dense(a):
        columns = lax.broadcasted_iota(jnp.int32, (128, TOK), 0) + a * 128

        def spread(step, total):
            at = pl.multiple_of(step * 8, 8)
            slot_rows, weight_rows = slot_t[pl.ds(at, 8), :], weight_t[pl.ds(at, 8), :]
            for u in range(8):
                hit = columns == slot_rows[u : u + 1, :]
                total = total + jnp.where(hit, weight_rows[u : u + 1, :], 0.0)
            return total

        total = lax.fori_loop(0, PICKS // 8, spread, jnp.zeros((128, TOK), F32))
        dense_t[pl.ds(a * 128, 128), :] = total.astype(BF16)

    for one in tables:
        one.wait()
    dense(0)
    z_step(1, 0)
    dense(1)
    c_step(2)
    dense(2)
    z_step(1, 1)
    dense(3)

    lane = lax.broadcasted_iota(jnp.int32, (TOK, TOK), 1)
    row = lax.broadcasted_iota(jnp.int32, (TOK, TOK), 0)
    owner = [route[0:1, :], route[1:2, :]]
    number = lax.broadcasted_iota(jnp.int32, (Z * Y, TOK), 0)
    hits = [jnp.where(number == one, 1.0, 0.0) for one in owner]
    earlier = jnp.where(row < lane, 1.0, 0.0).astype(BF16)
    ranks = [jnp.dot(hit.astype(BF16), earlier, preferred_element_type=F32) for hit in hits]
    ranks[1] = ranks[1] + jnp.sum(hits[0], axis=1, keepdims=True)
    ranks = [
        jnp.sum(hit * rank, axis=0, keepdims=True).astype(jnp.int32)
        for hit, rank in zip(hits, ranks)
    ]

    slot_ids = lax.broadcasted_iota(jnp.int32, (SLOTS, TOK), 0)
    for to in range(Y):
        total = jnp.zeros((SLOTS, ROWS), F32)
        lanes = []
        for j in range(2):
            here, group = owner[j] % Y == to, owner[j] // Y
            place = jnp.where(here, group * CAP + ranks[j], -1)
            one = jnp.where(slot_ids == place, 1.0, 0.0).astype(BF16)
            ps[j, pl.ds(to * SLOTS, SLOTS), :] = one
            total = total + lax.dot_general(
                one, dense_t[pl.ds(j * ROWS, ROWS), :], NT, preferred_element_type=F32
            )
            spot = group * (2 * CAP) + ranks[j] + (y % 2) * CAP
            lanes.append(jnp.where(here, spot, -1).astype(F32))
        wm[to, pl.ds(0, SLOTS), :] = total.astype(BF16)
        wm[to, pl.ds(SLOTS, 16), :] = jnp.broadcast_to(
            jnp.concatenate(lanes, axis=1), (16, ROWS)
        ).astype(BF16)
    for dy in (1, 3, 2):
        send(wm.at[(y + dy) % Y], wa.at[c, y], w1[dy], dev(dy=dy))
    wa[c, y] = wm[y]
    w_piece(0)

    c_step(4)
    c_step(3)
    z_step(2, 0)
    c_step(5)
    y_step(0)
    y_step(1)
    z_step(2, 1)
    c_step(6)
    c_step(7)
    w_piece(1)
    w_piece(3)
    z_step(3, 0)
    w_piece(2)
    y_step(2)
    z_step(3, 1)
    y_step(4)
    w_pass(1, 0)
    w_pass(3, 0)
    w_pass(2, 0)
    z_step(4, 0)
    y_step(3)
    w_last(0)
    z_step(4, 1)
    y_step(5)

    def prepare(i):
        src = source(i)

        def half(yp, carry):
            pi = (src % K) * 8 + (src // K) * 2 + yp
            slots = lax.broadcasted_iota(jnp.int32, (ROWS, TOK), 0).astype(F32)
            at = pl.multiple_of(pi * 16, 16)
            parts = []
            for q in range(2):
                row = wa[src, yp * 2 + q, pl.ds(SLOTS, 16), :].astype(F32)[0:1, :]
                hit = jnp.where(slots == row[:, :TOK], 1.0, 0.0)
                hit = hit + jnp.where(slots == row[:, TOK:], 1.0, 0.0)
                pm[pi, :, pl.ds(q * TOK, TOK)] = hit.astype(BF16)
                part = wa[src, yp * 2 + q, pl.ds(0, SLOTS), :].astype(F32)
                parts.append(part.reshape(Z, CAP, ROWS))
            wt[:, pl.ds(at, 16), :] = jnp.concatenate(parts, axis=1).astype(BF16)
            return carry

        lax.fori_loop(0, 2, half, 0)

    def gather(i):
        src = source(i)

        def half(yp, carry):
            pi = (src % K) * 8 + (src // K) * 2 + yp
            at = pl.multiple_of(pi * 16, 16)
            tokens = oga[src, pl.ds(yp * 2, 2)].reshape(2 * TOK, FEAT)
            got = jnp.dot(pm[pi], tokens, preferred_element_type=F32)
            gt[:, pl.ds(at, 16), :] = got.astype(BF16).reshape(Z, 16, FEAT)
            return carry

        lax.fori_loop(0, 2, half, 0)

    def p_step(s):
        def side(u, carry):
            at = (z + Z + (1 - 2 * u) * s) % Z
            rows = va[at].reshape(ROWS, FEAT)
            pt[at] = jnp.dot(wt[at], rows, preferred_element_type=F32).astype(BF16)
            return carry

        lax.fori_loop(0, 1 if s in (0, 8) else 2, side, 0)

    rid = ids.take(32)

    def grad_part(at, h):
        rows = pl.ds(h * HALF, HALF)
        return lax.dot_general(wt[at, :, rows], gt[at], TN, preferred_element_type=F32)

    def r_step(s, h):
        def stream(way, carry):
            at = (z + Z + (1 - 2 * way) * (8 - s)) % Z
            total = grad_part(at, h)
            if s >= 2:
                arrived(rz.at[s - 1, way, h], rid + (s - 1) * 4 + way * 2 + h)
                total = total + rz[s - 1, way, h].astype(F32)
            sz[s, way, h] = total.astype(BF16)
            if s == 1:

                @pl.when(way == h)
                def _():
                    arrived(rz.at[0, way, h], rid + way * 2 + h)
                    more = total + rz[0, way, h].astype(F32)
                    sz[s, way, h] = more.astype(BF16)

            to_mem = ((z + Z + 1 - 2 * way) % Z) * Y + y
            copy(
                sz.at[s, way, h], rz.at[s, way, h], rid + s * 4 + way * 2 + h, (dp, to_mem)
            ).start()
            return carry

        if s == 0:
            stream(h, 0)
        else:
            lax.fori_loop(0, 2, stream, 0)

    def r_last(h):
        total = grad_part(z, h)
        for way in range(2):
            arrived(rz.at[7, way, h], rid + 28 + way * 2 + h)
            total = total + rz[7, way, h].astype(F32)
        gv_v[pl.ds(h * HALF, HALF), :] = total
        part = pl.ds(h * HALF, HALF)
        done = pltpu.make_async_copy(gv_v.at[part], gv.at[part], lsem.at[h])
        done.start()
        return done

    def r_drain():
        def drain(i, carry):
            block = sz.at[i // 4, (i // 2) % 2, i % 2]

            @pl.when((i != 1) & (i != 2))
            def _():
                copy(block, block, rid + i, dev(dz=1)).wait_send()

            return carry

        lax.fori_loop(0, 32, drain, 0)

    i1 = ids.take()
    i2 = [ids.take() for _ in range(4)]
    i3 = [ids.take() for _ in range(4)]
    m1r = [ids.take() for _ in range(4)]
    m1l = [ids.take() for _ in range(4)]
    mr = [ids.take() for _ in range(8)]
    ml = [ids.take() for _ in range(8)]
    oid = [ids.take() for _ in order]
    far, up, down = (y + 2) % Y, (y + 1) % Y, (y + Y - 1) % Y
    couples = [(6, 7), (2, 3), (4, 5), (0, 1)]

    def to_of(i):
        dx, dk = order[i]
        return cof(dx, dk)

    def scatter(i):
        src = to_of(i)

        def half(yp, carry):
            pi = (src % K) * 8 + (src // K) * 2 + yp
            at = pl.multiple_of(pi * 16, 16)
            parts = pt[:, pl.ds(at, 16), :].reshape(ROWS, FEAT)
            got = lax.dot_general(pm[pi], parts, TN, preferred_element_type=F32)
            outp[src, pl.ds(yp * 2, 2)] = got.astype(BF16).reshape(2, TOK, FEAT)
            return carry

        lax.fori_loop(0, 2, half, 0)

    def m_first(n):
        e, o = couples[n]
        scatter(e)
        send(outp.at[to_of(e), far], ytr.at[n], m1r[n], dev(dy=1))
        send(outp.at[to_of(e), down], yfl.at[e], ml[e], dev(dy=Y - 1))
        scatter(o)
        send(outp.at[to_of(o), far], ytl.at[n], m1l[n], dev(dy=Y - 1))
        send(outp.at[to_of(o), up], yfr.at[o], mr[o], dev(dy=1))

    def m_second(n):
        e, o = couples[n]
        at = to_of(e)
        arrived(ytr.at[n], m1r[n])
        outp[at, up] = (outp[at, up].astype(F32) + ytr[n].astype(F32)).astype(BF16)
        send(outp.at[at, up], yfr.at[e], mr[e], dev(dy=1))
        at = to_of(o)
        arrived(ytl.at[n], m1l[n])
        outp[at, down] = (outp[at, down].astype(F32) + ytl[n].astype(F32)).astype(BF16)
        send(outp.at[at, down], yfl.at[o], ml[o], dev(dy=Y - 1))

    def m_final(n):
        for i in couples[n]:
            dx, dk = order[i]
            to = to_of(i)
            arrived(yfr.at[i], mr[i])
            arrived(yfl.at[i], ml[i])
            total = outp[to, y].astype(F32) + yfr[i].astype(F32) + yfl[i].astype(F32)
            outp[to, y] = total.astype(BF16)
            if i == 0:
                own = pltpu.make_async_copy(outp.at[to, y], out.at[:, cols(c)], lsem.at[3])
                own.start()
                own.wait()
            else:
                send(outp.at[to, y], out.at[:, cols(c)], oid[i], dev(dx=dx, dk=dk))

    def inner(at, carry):
        rows = va[at].reshape(ROWS, FEAT)
        got = lax.dot_general(gt[at], rows, NT, preferred_element_type=F32)
        ip[:, :, at] = got.astype(BF16).reshape(K, X, 32, ROWS)
        return carry

    def add_core(i, carry):
        xx = i // 4
        at = pl.ds((i % 4) * 4, 4)
        ic[xx, at] = (ip[k, xx, at].astype(F32) + ir[xx, at].astype(F32)).astype(BF16)
        return carry

    def add_chips(at, carry):
        total = ic[x, at].astype(F32)
        for i in range(3):
            total = total + ix[i, at].astype(F32)
        for q in range(4):
            iy[q, at] = total[q * CAP : (q + 1) * CAP, :]
        return carry

    for dy in (1, 3, 2):
        w_pass(1, dy)
        w_pass(3, dy)
    z_step(5, 0)
    for dy in (1, 3, 2):
        w_pass(2, dy)
    prepare(0)
    prepare(1)
    y_step(6)
    y_step(7)
    z_step(5, 1)
    prepare(2)
    prepare(4)
    y_last(0)
    gather(0)
    y_last(1)
    gather(1)
    z_step(6, 0)
    prepare(6)
    w_last(1)
    w_last(3)
    prepare(3)
    prepare(5)
    y_last(2)
    gather(2)
    w_last(2)
    prepare(7)
    z_step(6, 1)
    for step in range(4):
        p_step(step)
    y_last(3)
    gather(3)
    y_last(4)
    gather(4)
    z_step(7, 0)
    p_step(4)
    p_step(5)
    y_last(5)
    gather(5)
    for i in (6, 7):
        y_last(i)
        gather(i)
    r_step(0, 0)
    z_step(7, 1)
    r_step(0, 1)
    p_step(6)
    z_step(8, 0)
    p_step(7)
    z_step(8, 1)
    p_step(8)
    m_first(0)
    m_first(1)
    r_step(1, 0)
    r_step(1, 1)
    lax.fori_loop(0, Z // 2, inner, 0)
    r_step(2, 0)
    m_second(0)
    m_first(2)
    r_step(2, 1)
    lax.fori_loop(Z // 2, Z, inner, 0)
    send(ip.at[(k + 1) % K], ir, i1, dev(dk=1))
    r_step(3, 0)
    m_second(1)
    m_first(3)
    r_step(3, 1)
    arrived(ir, i1)
    lax.fori_loop(0, 16, add_core, 0)
    for dx in (1, 3, 2):
        send(ic.at[(x + dx) % X], ix.at[dx - 1], i2[dx], dev(dx=dx))
    r_step(4, 0)
    m_final(0)
    r_step(4, 1)
    m_second(2)
    r_step(5, 0)
    r_step(5, 1)
    m_final(1)
    r_step(6, 0)
    m_second(3)
    for dx in (1, 3, 2):
        arrived(ix.at[dx - 1], i2[dx])
    lax.fori_loop(0, Z, add_chips, 0)
    for q in range(4):
        isrc[4, pl.ds(q * SLOTS, SLOTS), :] = iy[q].reshape(SLOTS, ROWS).astype(BF16)
    isrc[0, pl.ds(0, SLOTS), :] = isrc[4, pl.ds(pl.multiple_of(y * SLOTS, SLOTS), SLOTS), :]
    for i in range(1, 4):
        to = (y + i) % Y
        send(
            isrc.at[4, pl.ds(pl.multiple_of(to * SLOTS, SLOTS), SLOTS), :],
            isrc.at[i, pl.ds(0, SLOTS), :], i3[i], dev(dy=i),
        )
    r_step(6, 1)
    r_step(7, 0)
    m_final(2)
    r_step(7, 1)
    for i in range(1, 4):
        arrived(isrc.at[i, pl.ds(0, SLOTS), :], i3[i])
    for j in range(2):
        total = jnp.zeros((TOK, ROWS), F32)
        for i in range(4):
            at = pl.multiple_of(((y + Y - i) % Y) * SLOTS, SLOTS)
            total = total + lax.dot_general(
                ps[j, pl.ds(at, SLOTS), :], isrc[i, pl.ds(0, SLOTS), :], TN,
                preferred_element_type=F32,
            )
        pair_v[:, pl.ds(j * ROWS, ROWS)] = total
    pair_out = pltpu.make_async_copy(pair_v, pair, lsem.at[6])
    pair_out.start()
    m_final(3)
    gv_done = [r_last(0)]
    for i in range(1, 8):
        arrived(out.at[:, cols(source(i))], oid[i])
    gv_done.append(r_last(1))
    pair_out.wait()
    for one in sent:
        one.wait_send()
    r_drain()
    for one in gv_done:
        one.wait()
    assert ids.count <= SEMS, ids.count


SEMS = 192


def pick(
    pair_in, slot_in, out_in, gv_in, out_ref, out_out, gv_out,
    pair_v, slot_v, picked, out_v, gv_v, fetch_sem, put_sem,
):
    number = 8
    blocks = [(pair_in, pair_v, None), (slot_in, slot_v, None)]
    for n in range(number):
        part = pl.ds(n * TOK // number, TOK // number)
        blocks.append((out_in.at[part], out_v.at[part], out_out.at[part]))
    for n in range(4):
        part = pl.ds(n * ROWS // 4, ROWS // 4)
        blocks.append((gv_in.at[part], gv_v.at[part], gv_out.at[part]))
    fetch = [
        pltpu.make_async_copy(src, held, fetch_sem.at[n])
        for n, (src, held, _) in enumerate(blocks)
    ]
    put = [
        pltpu.make_async_copy(held, dst, put_sem.at[n])
        for n, (_, held, dst) in enumerate(blocks)
        if dst is not None
    ]
    for one in fetch:
        one.start()
    fetch[0].wait()
    fetch[1].wait()
    slot = slot_v[...].T
    low, high = slot & 127, slot // 128
    total = jnp.zeros((TOK, PICKS), F32)
    for a in range(4):
        part = jnp.take_along_axis(pair_v[:, pl.ds(a * 128, 128)], low, axis=1)
        total = jnp.where(high == a, part, total)
    picked[...] = total.T
    last = pltpu.make_async_copy(picked, out_ref, put_sem.at[0])
    last.start()
    for one, two in zip(fetch[2:], put):
        one.wait()
        two.start()
    for one in put:
        one.wait()
    last.wait()


def shards(lookup_slot, lookup_weight, owner_route, values, out_grad):
    slot_t = lookup_slot.transpose(1, 2, 0).reshape(PICKS, TOK)
    weight_t = lookup_weight.transpose(1, 2, 0).reshape(PICKS, TOK)
    hbm = pl.BlockSpec(memory_space=pltpu.HBM)
    vmem, anywhere = pl.BlockSpec(memory_space=pltpu.VMEM), pl.BlockSpec(memory_space=pl.ANY)
    out, gv, pair = pl.pallas_call(
        exchange,
        out_shape=(
            jax.ShapeDtypeStruct((TOK, C * FEAT), BF16),
            jax.ShapeDtypeStruct((ROWS, FEAT), F32),
            jax.ShapeDtypeStruct((TOK, 2 * ROWS), F32),
        ),
        in_specs=[anywhere] * 5,
        out_specs=(anywhere, anywhere, anywhere),
        scratch_shapes=[
            pltpu.VMEM((Z, 2, HALF, FEAT), BF16),
            pltpu.VMEM((C, Y, TOK, FEAT), BF16),
            pltpu.VMEM((Y, MSG, ROWS), BF16),
            pltpu.VMEM((C, Y, MSG, ROWS), BF16),
            pltpu.VMEM((2, Y * SLOTS, TOK), BF16),
            pltpu.VMEM((2 * ROWS, TOK), BF16),
            pltpu.VMEM((PICKS, TOK), jnp.int32),
            pltpu.VMEM((PICKS, TOK), F32),
            pltpu.VMEM((2, TOK), jnp.int32),
            pltpu.VMEM((TOK, 2 * ROWS), F32),
            pltpu.VMEM((ROWS, FEAT), F32),
            pltpu.VMEM((16, ROWS, 2 * TOK), BF16),
            pltpu.VMEM((Z, 16 * 16, ROWS), BF16),
            pltpu.VMEM((Z, 16 * 16, FEAT), BF16),
            pltpu.VMEM((Z, 16 * 16, FEAT), BF16),
            pltpu.VMEM((K, X, Z, 32, ROWS), BF16),
            pltpu.VMEM((X, Z, 32, ROWS), BF16),
            pltpu.VMEM((X, Z, 32, ROWS), BF16),
            pltpu.VMEM((3, Z, 32, ROWS), BF16),
            pltpu.VMEM((4, Z, CAP, ROWS), F32),
            pltpu.VMEM((5, Y * SLOTS, ROWS), BF16),
            pltpu.VMEM((C, Y, TOK, FEAT), BF16),
            pltpu.VMEM((4, TOK, FEAT), BF16),
            pltpu.VMEM((4, TOK, FEAT), BF16),
            pltpu.VMEM((C, TOK, FEAT), BF16),
            pltpu.VMEM((C, TOK, FEAT), BF16),
            pltpu.VMEM((8, 2, 2, HALF, FEAT), BF16),
            pltpu.VMEM((8, 2, 2, HALF, FEAT), BF16),
            pltpu.SemaphoreType.DMA((SEMS,)),
            pltpu.SemaphoreType.DMA((SEMS,)),
            pltpu.SemaphoreType.DMA((8,)),
        ],
        compiler_params=pltpu.CompilerParams(
            collective_id=0, has_side_effects=True, vmem_limit_bytes=58 * 1024 * 1024
        ),
        name="exchange",
    )(slot_t, weight_t, owner_route.T, out_grad, values)
    grad_weight, out, gv = pl.pallas_call(
        pick,
        out_shape=(
            jax.ShapeDtypeStruct((PICKS, TOK), F32),
            jax.ShapeDtypeStruct(out.shape, out.dtype),
            jax.ShapeDtypeStruct(gv.shape, gv.dtype),
        ),
        in_specs=[hbm] * 4,
        out_specs=(hbm, hbm, hbm),
        scratch_shapes=[
            pltpu.VMEM((TOK, 2 * ROWS), F32),
            pltpu.VMEM((PICKS, TOK), jnp.int32),
            pltpu.VMEM((PICKS, TOK), F32),
            pltpu.VMEM((TOK, C * FEAT), BF16),
            pltpu.VMEM((ROWS, FEAT), F32),
            pltpu.SemaphoreType.DMA((14,)),
            pltpu.SemaphoreType.DMA((14,)),
        ],
        name="pick",
    )(pair, slot_t, out, gv)
    return out, gv, grad_weight.reshape(4, 32, TOK).transpose(2, 0, 1)


def solution(mesh):
    return jax.shard_map(
        shards,
        mesh=mesh,
        in_specs=(
            P(("dp", "mem"), None, None),
            P(("dp", "mem"), None, None),
            P(("dp", "mem"), None),
            P("mem", None),
            P(("dp", "mem"), None),
        ),
        out_specs=(P(("dp", "mem"), None), P("mem", "dp"), P(("dp", "mem"), None, None)),
        check_vma=False,
    )
```

```python
import functools

import jax
import jax.numpy as jnp
from jax import lax
from jax.experimental import pallas as pl
from jax.experimental.pallas import tpu as pltpu
from jax.sharding import PartitionSpec as P

MESH = pl.DeviceIdType.MESH
X, K, Z, Y = 4, 2, 16, 4
C = X * K
TOK, PICKS, ROWS, FEAT, CAP = 128, 128, 256, 512, 8
HALF = ROWS // 2
SLOTS = Z * CAP
MSG = SLOTS + 16
F32, BF16 = jnp.float32, jnp.bfloat16
NT = (((1,), (1,)), ((), ()))
TN = (((0,), (0,)), ((), ()))


class Ids:
    def __init__(self):
        self.count = 0

    def take(self, number=1):
        first = self.count
        self.count += number
        return first


def exchange(
    slot_in, weight_in, route_in, og, values,
    out, gv, pair,
    va, oga, wm, wa, ps, dense_t, slot_t, weight_t, route, pair_v, gv_v, pm, wt, gt, pt, ip, ir, ic, ix, iy, isrc,
    outp, ytr, ytl, yfr, yfl, rz, sz, ssem, rsem, lsem,
):
    dp, mem = lax.axis_index("dp"), lax.axis_index("mem")
    x, k = dp // K, dp % K
    z, y = mem // Y, mem % Y
    ids = Ids()
    sent = []

    def dev(dx=0, dk=0, dz=0, dy=0):
        to_dp = ((x + dx) % X) * K + (k + dk) % K
        to_mem = ((z + dz) % Z) * Y + (y + dy) % Y
        return (to_dp, to_mem)

    def cof(dx, dk):
        return ((x + dx) % X) * K + (k + dk) % K

    def copy(src, dst, sem, to):
        return pltpu.make_async_remote_copy(
            src_ref=src, dst_ref=dst, send_sem=ssem.at[sem], recv_sem=rsem.at[sem],
            device_id=to, device_id_type=MESH,
        )

    def send(src, dst, sem, to):
        one = copy(src, dst, sem, to)
        one.start()
        sent.append(one)

    def arrived(dst, sem):
        copy(dst, dst, sem, dev(dk=1)).wait_recv()

    def cols(index):
        return pl.ds(pl.multiple_of(index * FEAT, FEAT), FEAT)

    c = dp
    own_v = [
        pltpu.make_async_copy(
            values.at[pl.ds(h * HALF, HALF), cols(c)], va.at[z, h], lsem.at[h]
        )
        for h in range(2)
    ]
    for one in own_v:
        one.start()
    own_og = pltpu.make_async_copy(og.at[:, cols(c)], oga.at[c, y], lsem.at[2])
    own_og.start()
    tables = [
        pltpu.make_async_copy(slot_in, slot_t, lsem.at[4]),
        pltpu.make_async_copy(weight_in, weight_t, lsem.at[5]),
        pltpu.make_async_copy(route_in, route, lsem.at[7]),
    ]
    for one in tables:
        one.start()

    barrier = pltpu.get_barrier_semaphore()
    others = [(dx, dk) for dx in range(X) for dk in range(K) if (dx, dk) != (0, 0)]
    partners = [dev(dz=1), dev(dz=Z - 1)] + [dev(dy=d) for d in range(1, Y)]
    partners += [dev(dx=dx, dk=dk) for dx, dk in others]
    for partner in partners:
        pl.semaphore_signal(barrier, inc=1, device_id=partner, device_id_type=MESH)
    pl.semaphore_wait(barrier, len(partners))

    hops = {("r", 0): 8, ("l", 0): 7, ("r", 1): 7, ("l", 1): 8}
    zid = {(key, s): ids.take() for key, n in hops.items() for s in range(1, n + 1)}

    def z_send(s, way, h):
        if s <= hops[way, h]:
            if way == "r":
                at, to = (z + Z - s + 1) % Z, dev(dz=1)
            else:
                at, to = (z + s - 1) % Z, dev(dz=Z - 1)
            block = values.at[pl.ds(h * HALF, HALF), cols(c)] if s == 1 else va.at[at, h]
            send(block, va.at[at, h], zid[((way, h), s)], to)

    def z_step(s, h):
        for way in ("r", "l"):
            if s <= hops[way, h]:
                at = (z + Z - s) % Z if way == "r" else (z + s) % Z
                arrived(va.at[at, h], zid[((way, h), s)])
                z_send(s + 1, way, h)

    order = [(0, 0), (0, 1), (1, 0), (1, 1), (3, 0), (3, 1), (2, 0), (2, 1)]
    cid = [ids.take() for _ in order]
    yr1 = [ids.take() for _ in order]
    yl1 = [ids.take() for _ in order]
    y2 = [ids.take() for _ in order]

    def c_send(i):
        dx, dk = order[i]
        to = cof(dx, dk)
        send(og.at[:, cols(to)], oga.at[c, y], cid[i], dev(dx=dx, dk=dk))

    def source(i):
        dx, dk = order[i]
        return cof(X - dx, dk)

    def y_send(i):
        held = oga.at[source(i), y]
        block = held if i else og.at[:, cols(c)]
        send(block, held, yr1[i], dev(dy=1))
        send(block, held, yl1[i], dev(dy=Y - 1))

    def c_step(i):
        arrived(oga.at[source(i), y], cid[i])
        y_send(i)

    def y_step(i):
        right = oga.at[source(i), (y + Y - 1) % Y]
        left = oga.at[source(i), (y + 1) % Y]
        if i % 2 == 0:
            arrived(right, yr1[i])
            send(right, right, y2[i], dev(dy=1))
            arrived(left, yl1[i])
        else:
            arrived(left, yl1[i])
            send(left, left, y2[i], dev(dy=Y - 1))
            arrived(right, yr1[i])

    def y_last(i):
        arrived(oga.at[source(i), (y + 2) % Y], y2[i])

    w1 = [ids.take() for _ in range(Y)]
    w2 = {(dx, dy): ids.take() for dx in range(X) for dy in range(Y)}
    w3 = {(dx, dy): ids.take() for dx in range(1, X) for dy in range(Y)}

    def w_piece(dy):
        at = (y + Y - dy) % Y
        if dy:
            arrived(wa.at[c, at], w1[dy])
        for dx in (1, 3, 2):
            send(wa.at[c, at], wa.at[c, at], w2[dx, dy], dev(dx=dx))
        send(wa.at[c, at], wa.at[c, at], w2[0, dy], dev(dk=1))

    def w_pass(dx, dy):
        block = wa.at[cof(X - dx, 0), (y + Y - dy) % Y]
        arrived(block, w2[dx, dy])
        send(block, block, w3[dx, dy], dev(dk=1))

    def w_last(dx):
        for dy in range(Y):
            block = wa.at[cof(X - dx, 1), (y + Y - dy) % Y]
            arrived(block, w3[dx, dy] if dx else w2[0, dy])

    for way, h in hops:
        z_send(1, way, h)
    for i in range(1, 8):
        c_send(i)
    y_send(0)
    c_step(1)

    def dense(a):
        columns = lax.broadcasted_iota(jnp.int32, (128, TOK), 0) + a * 128

        def spread(step, total):
            at = pl.multiple_of(step * 8, 8)
            slot_rows, weight_rows = slot_t[pl.ds(at, 8), :], weight_t[pl.ds(at, 8), :]
            for u in range(8):
                hit = columns == slot_rows[u : u + 1, :]
                total = total + jnp.where(hit, weight_rows[u : u + 1, :], 0.0)
            return total

        total = lax.fori_loop(0, PICKS // 8, spread, jnp.zeros((128, TOK), F32))
        dense_t[pl.ds(a * 128, 128), :] = total.astype(BF16)

    for one in tables:
        one.wait()
    dense(0)
    z_step(1, 0)
    dense(1)
    c_step(2)
    dense(2)
    z_step(1, 1)
    dense(3)

    lane = lax.broadcasted_iota(jnp.int32, (TOK, TOK), 1)
    row = lax.broadcasted_iota(jnp.int32, (TOK, TOK), 0)
    owner = [route[0:1, :], route[1:2, :]]
    number = lax.broadcasted_iota(jnp.int32, (Z * Y, TOK), 0)
    hits = [jnp.where(number == one, 1.0, 0.0) for one in owner]
    earlier = jnp.where(row < lane, 1.0, 0.0).astype(BF16)
    ranks = [jnp.dot(hit.astype(BF16), earlier, preferred_element_type=F32) for hit in hits]
    ranks[1] = ranks[1] + jnp.sum(hits[0], axis=1, keepdims=True)
    ranks = [
        jnp.sum(hit * rank, axis=0, keepdims=True).astype(jnp.int32)
        for hit, rank in zip(hits, ranks)
    ]

    slot_ids = lax.broadcasted_iota(jnp.int32, (SLOTS, TOK), 0)
    for to in range(Y):
        total = jnp.zeros((SLOTS, ROWS), F32)
        lanes = []
        for j in range(2):
            here, group = owner[j] % Y == to, owner[j] // Y
            place = jnp.where(here, group * CAP + ranks[j], -1)
            one = jnp.where(slot_ids == place, 1.0, 0.0).astype(BF16)
            ps[j, pl.ds(to * SLOTS, SLOTS), :] = one
            total = total + lax.dot_general(
                one, dense_t[pl.ds(j * ROWS, ROWS), :], NT, preferred_element_type=F32
            )
            spot = group * (2 * CAP) + ranks[j] + (y % 2) * CAP
            lanes.append(jnp.where(here, spot, -1).astype(F32))
        wm[to, pl.ds(0, SLOTS), :] = total.astype(BF16)
        wm[to, pl.ds(SLOTS, 16), :] = jnp.broadcast_to(
            jnp.concatenate(lanes, axis=1), (16, ROWS)
        ).astype(BF16)
    for dy in (1, 3, 2):
        send(wm.at[(y + dy) % Y], wa.at[c, y], w1[dy], dev(dy=dy))
    wa[c, y] = wm[y]
    w_piece(0)

    c_step(4)
    c_step(3)
    z_step(2, 0)
    c_step(5)
    y_step(0)
    y_step(1)
    z_step(2, 1)
    c_step(6)
    c_step(7)
    w_piece(1)
    w_piece(3)
    z_step(3, 0)
    w_piece(2)
    y_step(2)
    z_step(3, 1)
    y_step(4)
    w_pass(1, 0)
    w_pass(3, 0)
    w_pass(2, 0)
    z_step(4, 0)
    y_step(3)
    w_last(0)
    z_step(4, 1)
    y_step(5)

    def prepare(i):
        src = source(i)

        def half(yp, carry):
            pi = (src % K) * 8 + (src // K) * 2 + yp
            slots = lax.broadcasted_iota(jnp.int32, (ROWS, TOK), 0).astype(F32)
            at = pl.multiple_of(pi * 16, 16)
            parts = []
            for q in range(2):
                row = wa[src, yp * 2 + q, pl.ds(SLOTS, 16), :].astype(F32)[0:1, :]
                hit = jnp.where(slots == row[:, :TOK], 1.0, 0.0)
                hit = hit + jnp.where(slots == row[:, TOK:], 1.0, 0.0)
                pm[pi, :, pl.ds(q * TOK, TOK)] = hit.astype(BF16)
                part = wa[src, yp * 2 + q, pl.ds(0, SLOTS), :].astype(F32)
                parts.append(part.reshape(Z, CAP, ROWS))
            wt[:, pl.ds(at, 16), :] = jnp.concatenate(parts, axis=1).astype(BF16)
            return carry

        lax.fori_loop(0, 2, half, 0)

    def gather(i):
        src = source(i)

        def half(yp, carry):
            pi = (src % K) * 8 + (src // K) * 2 + yp
            at = pl.multiple_of(pi * 16, 16)
            tokens = oga[src, pl.ds(yp * 2, 2)].reshape(2 * TOK, FEAT)
            got = jnp.dot(pm[pi], tokens, preferred_element_type=F32)
            gt[:, pl.ds(at, 16), :] = got.astype(BF16).reshape(Z, 16, FEAT)
            return carry

        lax.fori_loop(0, 2, half, 0)

    def p_step(s):
        def side(u, carry):
            at = (z + Z + (1 - 2 * u) * s) % Z
            rows = va[at].reshape(ROWS, FEAT)
            pt[at] = jnp.dot(wt[at], rows, preferred_element_type=F32).astype(BF16)
            return carry

        lax.fori_loop(0, 1 if s in (0, 8) else 2, side, 0)

    rid = ids.take(32)

    def grad_part(at, h):
        rows = pl.ds(h * HALF, HALF)
        return lax.dot_general(wt[at, :, rows], gt[at], TN, preferred_element_type=F32)

    def r_step(s, h):
        def stream(way, carry):
            at = (z + Z + (1 - 2 * way) * (8 - s)) % Z
            total = grad_part(at, h)
            if s >= 2:
                arrived(rz.at[s - 1, way, h], rid + (s - 1) * 4 + way * 2 + h)
                total = total + rz[s - 1, way, h].astype(F32)
            sz[s, way, h] = total.astype(BF16)
            if s == 1:

                @pl.when(way == h)
                def _():
                    arrived(rz.at[0, way, h], rid + way * 2 + h)
                    more = total + rz[0, way, h].astype(F32)
                    sz[s, way, h] = more.astype(BF16)

            to_mem = ((z + Z + 1 - 2 * way) % Z) * Y + y
            copy(
                sz.at[s, way, h], rz.at[s, way, h], rid + s * 4 + way * 2 + h, (dp, to_mem)
            ).start()
            return carry

        if s == 0:
            stream(h, 0)
        else:
            lax.fori_loop(0, 2, stream, 0)

    def r_last(h):
        total = grad_part(z, h)
        for way in range(2):
            arrived(rz.at[7, way, h], rid + 28 + way * 2 + h)
            total = total + rz[7, way, h].astype(F32)
        gv_v[pl.ds(h * HALF, HALF), :] = total
        part = pl.ds(h * HALF, HALF)
        done = pltpu.make_async_copy(gv_v.at[part], gv.at[part], lsem.at[h])
        done.start()
        return done

    def r_drain(first, last):
        def drain(i, carry):
            block = sz.at[i // 4, (i // 2) % 2, i % 2]

            @pl.when((i != 1) & (i != 2))
            def _():
                copy(block, block, rid + i, dev(dz=1)).wait_send()

            return carry

        lax.fori_loop(first, last, drain, 0)

    i1 = ids.take()
    i2 = [ids.take() for _ in range(4)]
    i3 = [ids.take() for _ in range(4)]
    m1r = [ids.take() for _ in range(4)]
    m1l = [ids.take() for _ in range(4)]
    mr = [ids.take() for _ in range(8)]
    ml = [ids.take() for _ in range(8)]
    oid = [ids.take() for _ in order]
    far, up, down = (y + 2) % Y, (y + 1) % Y, (y + Y - 1) % Y
    couples = [(6, 7), (2, 3), (4, 5), (0, 1)]

    def to_of(i):
        dx, dk = order[i]
        return cof(dx, dk)

    def scatter(i):
        src = to_of(i)

        def half(yp, carry):
            pi = (src % K) * 8 + (src // K) * 2 + yp
            at = pl.multiple_of(pi * 16, 16)
            parts = pt[:, pl.ds(at, 16), :].reshape(ROWS, FEAT)
            got = lax.dot_general(pm[pi], parts, TN, preferred_element_type=F32)
            outp[src, pl.ds(yp * 2, 2)] = got.astype(BF16).reshape(2, TOK, FEAT)
            return carry

        lax.fori_loop(0, 2, half, 0)

    def m_first(n):
        e, o = couples[n]
        scatter(e)
        send(outp.at[to_of(e), far], ytr.at[n], m1r[n], dev(dy=1))
        send(outp.at[to_of(e), down], yfl.at[e], ml[e], dev(dy=Y - 1))
        scatter(o)
        send(outp.at[to_of(o), far], ytl.at[n], m1l[n], dev(dy=Y - 1))
        send(outp.at[to_of(o), up], yfr.at[o], mr[o], dev(dy=1))

    def m_second(n):
        e, o = couples[n]
        at = to_of(e)
        arrived(ytr.at[n], m1r[n])
        outp[at, up] = (outp[at, up].astype(F32) + ytr[n].astype(F32)).astype(BF16)
        send(outp.at[at, up], yfr.at[e], mr[e], dev(dy=1))
        at = to_of(o)
        arrived(ytl.at[n], m1l[n])
        outp[at, down] = (outp[at, down].astype(F32) + ytl[n].astype(F32)).astype(BF16)
        send(outp.at[at, down], yfl.at[o], ml[o], dev(dy=Y - 1))

    def m_final(n):
        for i in couples[n]:
            dx, dk = order[i]
            to = to_of(i)
            arrived(yfr.at[i], mr[i])
            arrived(yfl.at[i], ml[i])
            total = outp[to, y].astype(F32) + yfr[i].astype(F32) + yfl[i].astype(F32)
            outp[to, y] = total.astype(BF16)
            if i == 0:
                own = pltpu.make_async_copy(outp.at[to, y], out.at[:, cols(c)], lsem.at[3])
                own.start()
                own.wait()
            else:
                send(outp.at[to, y], out.at[:, cols(c)], oid[i], dev(dx=dx, dk=dk))

    def inner(at, carry):
        rows = va[at].reshape(ROWS, FEAT)
        got = lax.dot_general(gt[at], rows, NT, preferred_element_type=F32)
        ip[:, :, at] = got.astype(BF16).reshape(K, X, 32, ROWS)
        return carry

    def add_core(i, carry):
        xx = i // 4
        at = pl.ds((i % 4) * 4, 4)
        ic[xx, at] = (ip[k, xx, at].astype(F32) + ir[xx, at].astype(F32)).astype(BF16)
        return carry

    def add_chips(at, carry):
        total = ic[x, at].astype(F32)
        for i in range(3):
            total = total + ix[i, at].astype(F32)
        for q in range(4):
            iy[q, at] = total[q * CAP : (q + 1) * CAP, :]
        return carry

    for dy in (1, 3, 2):
        w_pass(1, dy)
        w_pass(3, dy)
    z_step(5, 0)
    for dy in (1, 3, 2):
        w_pass(2, dy)
    for one in own_v:
        one.wait()
    own_og.wait()
    prepare(0)
    prepare(1)
    y_step(6)
    y_step(7)
    z_step(5, 1)
    prepare(2)
    prepare(4)
    y_last(0)
    gather(0)
    y_last(1)
    gather(1)
    z_step(6, 0)
    prepare(6)
    w_last(1)
    w_last(3)
    prepare(3)
    prepare(5)
    y_last(2)
    gather(2)
    w_last(2)
    prepare(7)
    z_step(6, 1)
    for step in range(4):
        p_step(step)
    y_last(3)
    gather(3)
    y_last(4)
    gather(4)
    z_step(7, 0)
    p_step(4)
    p_step(5)
    y_last(5)
    gather(5)
    for i in (6, 7):
        y_last(i)
        gather(i)
    r_step(0, 0)
    z_step(7, 1)
    r_step(0, 1)
    p_step(6)
    z_step(8, 0)
    p_step(7)
    z_step(8, 1)
    p_step(8)
    early = len(sent)
    m_first(0)
    m_first(1)
    r_step(1, 0)
    r_step(1, 1)
    lax.fori_loop(0, Z // 2, inner, 0)
    r_step(2, 0)
    m_second(0)
    m_first(2)
    r_step(2, 1)
    lax.fori_loop(Z // 2, Z, inner, 0)
    send(ip.at[(k + 1) % K], ir, i1, dev(dk=1))
    r_step(3, 0)
    m_second(1)
    m_first(3)
    r_step(3, 1)
    arrived(ir, i1)
    lax.fori_loop(0, 16, add_core, 0)
    for dx in (1, 3, 2):
        send(ic.at[(x + dx) % X], ix.at[dx - 1], i2[dx], dev(dx=dx))
    r_step(4, 0)
    m_final(0)
    r_step(4, 1)
    m_second(2)
    r_step(5, 0)
    for one in sent[: early // 2]:
        one.wait_send()
    del sent[: early // 2]
    early -= early // 2
    r_step(5, 1)
    m_final(1)
    r_step(6, 0)
    m_second(3)
    for dx in (1, 3, 2):
        arrived(ix.at[dx - 1], i2[dx])
    lax.fori_loop(0, Z, add_chips, 0)
    for q in range(4):
        isrc[4, pl.ds(q * SLOTS, SLOTS), :] = iy[q].reshape(SLOTS, ROWS).astype(BF16)
    isrc[0, pl.ds(0, SLOTS), :] = isrc[4, pl.ds(pl.multiple_of(y * SLOTS, SLOTS), SLOTS), :]
    for i in range(1, 4):
        to = (y + i) % Y
        send(
            isrc.at[4, pl.ds(pl.multiple_of(to * SLOTS, SLOTS), SLOTS), :],
            isrc.at[i, pl.ds(0, SLOTS), :], i3[i], dev(dy=i),
        )
    r_step(6, 1)
    for one in sent[:early]:
        one.wait_send()
    del sent[:early]
    r_drain(0, 20)
    r_step(7, 0)
    m_final(2)
    r_step(7, 1)
    for i in range(1, 4):
        arrived(isrc.at[i, pl.ds(0, SLOTS), :], i3[i])
    for j in range(2):
        total = jnp.zeros((TOK, ROWS), F32)
        for i in range(4):
            at = pl.multiple_of(((y + Y - i) % Y) * SLOTS, SLOTS)
            total = total + lax.dot_general(
                ps[j, pl.ds(at, SLOTS), :], isrc[i, pl.ds(0, SLOTS), :], TN,
                preferred_element_type=F32,
            )
        pair_v[:, pl.ds(j * ROWS, ROWS)] = total
    pair_out = pltpu.make_async_copy(pair_v, pair, lsem.at[6])
    pair_out.start()
    m_final(3)
    gv_done = [r_last(0)]
    for i in range(1, 8):
        arrived(out.at[:, cols(source(i))], oid[i])
    gv_done.append(r_last(1))
    pair_out.wait()
    for one in sent:
        one.wait_send()
    r_drain(20, 32)
    for one in gv_done:
        one.wait()
    assert ids.count <= SEMS, ids.count


SEMS = 192


def pick(
    pair_in, slot_in, out_in, gv_in, out_ref, out_out, gv_out,
    pair_v, slot_v, picked, out_v, gv_v, fetch_sem, put_sem,
):
    number = 8
    blocks = [(pair_in, pair_v, None), (slot_in, slot_v, None)]
    for n in range(number):
        part = pl.ds(n * TOK // number, TOK // number)
        blocks.append((out_in.at[part], out_v.at[part], out_out.at[part]))
    for n in range(4):
        part = pl.ds(n * ROWS // 4, ROWS // 4)
        blocks.append((gv_in.at[part], gv_v.at[part], gv_out.at[part]))
    fetch = [
        pltpu.make_async_copy(src, held, fetch_sem.at[n])
        for n, (src, held, _) in enumerate(blocks)
    ]
    put = [
        pltpu.make_async_copy(held, dst, put_sem.at[n])
        for n, (_, held, dst) in enumerate(blocks)
        if dst is not None
    ]
    for one in fetch:
        one.start()
    fetch[0].wait()
    fetch[1].wait()
    slot = slot_v[...].T
    low, high = slot & 127, slot // 128
    total = jnp.zeros((TOK, PICKS), F32)
    for a in range(4):
        part = jnp.take_along_axis(pair_v[:, pl.ds(a * 128, 128)], low, axis=1)
        total = jnp.where(high == a, part, total)
    picked[...] = total.T
    last = pltpu.make_async_copy(picked, out_ref, put_sem.at[0])
    last.start()
    for one, two in zip(fetch[2:], put):
        one.wait()
        two.start()
    for one in put:
        one.wait()
    last.wait()


def shards(lookup_slot, lookup_weight, owner_route, values, out_grad):
    slot_t = lookup_slot.transpose(1, 2, 0).reshape(PICKS, TOK)
    weight_t = lookup_weight.transpose(1, 2, 0).reshape(PICKS, TOK)
    hbm = pl.BlockSpec(memory_space=pltpu.HBM)
    vmem, anywhere = pl.BlockSpec(memory_space=pltpu.VMEM), pl.BlockSpec(memory_space=pl.ANY)
    out, gv, pair = pl.pallas_call(
        exchange,
        out_shape=(
            jax.ShapeDtypeStruct((TOK, C * FEAT), BF16),
            jax.ShapeDtypeStruct((ROWS, FEAT), F32),
            jax.ShapeDtypeStruct((TOK, 2 * ROWS), F32),
        ),
        in_specs=[anywhere] * 5,
        out_specs=(anywhere, anywhere, anywhere),
        scratch_shapes=[
            pltpu.VMEM((Z, 2, HALF, FEAT), BF16),
            pltpu.VMEM((C, Y, TOK, FEAT), BF16),
            pltpu.VMEM((Y, MSG, ROWS), BF16),
            pltpu.VMEM((C, Y, MSG, ROWS), BF16),
            pltpu.VMEM((2, Y * SLOTS, TOK), BF16),
            pltpu.VMEM((2 * ROWS, TOK), BF16),
            pltpu.VMEM((PICKS, TOK), jnp.int32),
            pltpu.VMEM((PICKS, TOK), F32),
            pltpu.VMEM((2, TOK), jnp.int32),
            pltpu.VMEM((TOK, 2 * ROWS), F32),
            pltpu.VMEM((ROWS, FEAT), F32),
            pltpu.VMEM((16, ROWS, 2 * TOK), BF16),
            pltpu.VMEM((Z, 16 * 16, ROWS), BF16),
            pltpu.VMEM((Z, 16 * 16, FEAT), BF16),
            pltpu.VMEM((Z, 16 * 16, FEAT), BF16),
            pltpu.VMEM((K, X, Z, 32, ROWS), BF16),
            pltpu.VMEM((X, Z, 32, ROWS), BF16),
            pltpu.VMEM((X, Z, 32, ROWS), BF16),
            pltpu.VMEM((3, Z, 32, ROWS), BF16),
            pltpu.VMEM((4, Z, CAP, ROWS), F32),
            pltpu.VMEM((5, Y * SLOTS, ROWS), BF16),
            pltpu.VMEM((C, Y, TOK, FEAT), BF16),
            pltpu.VMEM((4, TOK, FEAT), BF16),
            pltpu.VMEM((4, TOK, FEAT), BF16),
            pltpu.VMEM((C, TOK, FEAT), BF16),
            pltpu.VMEM((C, TOK, FEAT), BF16),
            pltpu.VMEM((8, 2, 2, HALF, FEAT), BF16),
            pltpu.VMEM((8, 2, 2, HALF, FEAT), BF16),
            pltpu.SemaphoreType.DMA((SEMS,)),
            pltpu.SemaphoreType.DMA((SEMS,)),
            pltpu.SemaphoreType.DMA((8,)),
        ],
        compiler_params=pltpu.CompilerParams(
            collective_id=0, has_side_effects=True, vmem_limit_bytes=58 * 1024 * 1024
        ),
        name="exchange",
    )(slot_t, weight_t, owner_route.T, out_grad, values)
    grad_weight, out, gv = pl.pallas_call(
        pick,
        out_shape=(
            jax.ShapeDtypeStruct((PICKS, TOK), F32),
            jax.ShapeDtypeStruct(out.shape, out.dtype),
            jax.ShapeDtypeStruct(gv.shape, gv.dtype),
        ),
        in_specs=[hbm] * 4,
        out_specs=(hbm, hbm, hbm),
        scratch_shapes=[
            pltpu.VMEM((TOK, 2 * ROWS), F32),
            pltpu.VMEM((PICKS, TOK), jnp.int32),
            pltpu.VMEM((PICKS, TOK), F32),
            pltpu.VMEM((TOK, C * FEAT), BF16),
            pltpu.VMEM((ROWS, FEAT), F32),
            pltpu.SemaphoreType.DMA((14,)),
            pltpu.SemaphoreType.DMA((14,)),
        ],
        name="pick",
    )(pair, slot_t, out, gv)
    return out, gv, grad_weight.reshape(4, 32, TOK).transpose(2, 0, 1)


def solution(mesh):
    return jax.shard_map(
        shards,
        mesh=mesh,
        in_specs=(
            P(("dp", "mem"), None, None),
            P(("dp", "mem"), None, None),
            P(("dp", "mem"), None),
            P("mem", None),
            P(("dp", "mem"), None),
        ),
        out_specs=(P(("dp", "mem"), None), P("mem", "dp"), P(("dp", "mem"), None, None)),
        check_vma=False,
    )
```

```python
import functools

import jax
import jax.numpy as jnp
from jax import lax
from jax.experimental import pallas as pl
from jax.experimental.pallas import tpu as pltpu
from jax.sharding import PartitionSpec as P

MESH = pl.DeviceIdType.MESH
X, K, Z, Y = 4, 2, 16, 4
C = X * K
TOK, PICKS, ROWS, FEAT, CAP = 128, 128, 256, 512, 8
HALF = ROWS // 2
SLOTS = Z * CAP
MSG = SLOTS + 16
F32, BF16 = jnp.float32, jnp.bfloat16
NT = (((1,), (1,)), ((), ()))
TN = (((0,), (0,)), ((), ()))


class Ids:
    def __init__(self):
        self.count = 0

    def take(self, number=1):
        first = self.count
        self.count += number
        return first


def exchange(
    slot_in, weight_in, route_in, og, values,
    out, gv, pair,
    va, oga, wm, wa, ps, dense_t, slot_t, weight_t, route, pair_v, gv_v, pm, wt, gt, pt, ip, ir, ic, ix, iy, isrc,
    outp, ytr, ytl, yfr, yfl, rz, sz, ssem, rsem, lsem,
):
    dp, mem = lax.axis_index("dp"), lax.axis_index("mem")
    x, k = dp // K, dp % K
    z, y = mem // Y, mem % Y
    ids = Ids()
    sent = []

    def dev(dx=0, dk=0, dz=0, dy=0):
        to_dp = ((x + dx) % X) * K + (k + dk) % K
        to_mem = ((z + dz) % Z) * Y + (y + dy) % Y
        return (to_dp, to_mem)

    def cof(dx, dk):
        return ((x + dx) % X) * K + (k + dk) % K

    def copy(src, dst, sem, to):
        return pltpu.make_async_remote_copy(
            src_ref=src, dst_ref=dst, send_sem=ssem.at[sem], recv_sem=rsem.at[sem],
            device_id=to, device_id_type=MESH,
        )

    def send(src, dst, sem, to):
        one = copy(src, dst, sem, to)
        one.start()
        sent.append(one)

    def arrived(dst, sem):
        copy(dst, dst, sem, dev(dk=1)).wait_recv()

    def cols(index):
        return pl.ds(pl.multiple_of(index * FEAT, FEAT), FEAT)

    c = dp
    own_v = [
        pltpu.make_async_copy(
            values.at[pl.ds(h * HALF, HALF), cols(c)], va.at[z, h], lsem.at[h]
        )
        for h in range(2)
    ]
    for one in own_v:
        one.start()
    own_og = pltpu.make_async_copy(og.at[:, cols(c)], oga.at[c, y], lsem.at[2])
    own_og.start()
    tables = [
        pltpu.make_async_copy(slot_in, slot_t, lsem.at[4]),
        pltpu.make_async_copy(weight_in, weight_t, lsem.at[5]),
        pltpu.make_async_copy(route_in, route, lsem.at[7]),
    ]
    for one in tables:
        one.start()

    barrier = pltpu.get_barrier_semaphore()
    others = [(dx, dk) for dx in range(X) for dk in range(K) if (dx, dk) != (0, 0)]
    partners = [dev(dz=1), dev(dz=Z - 1)] + [dev(dy=d) for d in range(1, Y)]
    partners += [dev(dx=dx, dk=dk) for dx, dk in others]
    for partner in partners:
        pl.semaphore_signal(barrier, inc=1, device_id=partner, device_id_type=MESH)
    pl.semaphore_wait(barrier, len(partners))

    hops = {("r", 0): 8, ("l", 0): 7, ("r", 1): 7, ("l", 1): 8}
    zid = {(key, s): ids.take() for key, n in hops.items() for s in range(1, n + 1)}

    def z_send(s, way, h):
        if s <= hops[way, h]:
            if way == "r":
                at, to = (z + Z - s + 1) % Z, dev(dz=1)
            else:
                at, to = (z + s - 1) % Z, dev(dz=Z - 1)
            block = values.at[pl.ds(h * HALF, HALF), cols(c)] if s == 1 else va.at[at, h]
            send(block, va.at[at, h], zid[((way, h), s)], to)

    def z_step(s, h):
        for way in ("r", "l"):
            if s <= hops[way, h]:
                at = (z + Z - s) % Z if way == "r" else (z + s) % Z
                arrived(va.at[at, h], zid[((way, h), s)])
                z_send(s + 1, way, h)

    order = [(0, 0), (0, 1), (1, 0), (1, 1), (3, 0), (3, 1), (2, 0), (2, 1)]
    cid = [ids.take() for _ in order]
    yr1 = [ids.take() for _ in order]
    yl1 = [ids.take() for _ in order]
    y2 = [ids.take() for _ in order]

    def c_send(i):
        dx, dk = order[i]
        to = cof(dx, dk)
        send(og.at[:, cols(to)], oga.at[c, y], cid[i], dev(dx=dx, dk=dk))

    def source(i):
        dx, dk = order[i]
        return cof(X - dx, dk)

    def y_send(i):
        held = oga.at[source(i), y]
        block = held if i else og.at[:, cols(c)]
        send(block, held, yr1[i], dev(dy=1))
        send(block, held, yl1[i], dev(dy=Y - 1))

    def c_step(i):
        arrived(oga.at[source(i), y], cid[i])
        y_send(i)

    def y_step(i):
        right = oga.at[source(i), (y + Y - 1) % Y]
        left = oga.at[source(i), (y + 1) % Y]
        if i % 2 == 0:
            arrived(right, yr1[i])
            send(right, right, y2[i], dev(dy=1))
            arrived(left, yl1[i])
        else:
            arrived(left, yl1[i])
            send(left, left, y2[i], dev(dy=Y - 1))
            arrived(right, yr1[i])

    def y_last(i):
        arrived(oga.at[source(i), (y + 2) % Y], y2[i])

    w1 = [ids.take() for _ in range(Y)]
    w2 = {(dx, dy): ids.take() for dx in range(X) for dy in range(Y)}
    w3 = {(dx, dy): ids.take() for dx in range(1, X) for dy in range(Y)}

    def w_piece(dy):
        at = (y + Y - dy) % Y
        if dy:
            arrived(wa.at[c, at], w1[dy])
        for dx in (1, 3, 2):
            send(wa.at[c, at], wa.at[c, at], w2[dx, dy], dev(dx=dx))
        send(wa.at[c, at], wa.at[c, at], w2[0, dy], dev(dk=1))

    def w_pass(dx, dy):
        block = wa.at[cof(X - dx, 0), (y + Y - dy) % Y]
        arrived(block, w2[dx, dy])
        send(block, block, w3[dx, dy], dev(dk=1))

    def w_last(dx):
        for dy in range(Y):
            block = wa.at[cof(X - dx, 1), (y + Y - dy) % Y]
            arrived(block, w3[dx, dy] if dx else w2[0, dy])

    for way, h in hops:
        z_send(1, way, h)
    for i in range(1, 8):
        c_send(i)
    y_send(0)
    c_step(1)

    def dense(a):
        columns = lax.broadcasted_iota(jnp.int32, (128, TOK), 0) + a * 128

        def spread(step, total):
            at = pl.multiple_of(step * 8, 8)
            slot_rows, weight_rows = slot_t[pl.ds(at, 8), :], weight_t[pl.ds(at, 8), :]
            for u in range(8):
                hit = columns == slot_rows[u : u + 1, :]
                total = total + jnp.where(hit, weight_rows[u : u + 1, :], 0.0)
            return total

        total = lax.fori_loop(0, PICKS // 8, spread, jnp.zeros((128, TOK), F32))
        dense_t[pl.ds(a * 128, 128), :] = total.astype(BF16)

    for one in tables:
        one.wait()
    dense(0)
    z_step(1, 0)
    dense(1)
    c_step(2)
    dense(2)
    c_step(4)
    z_step(1, 1)
    dense(3)

    lane = lax.broadcasted_iota(jnp.int32, (TOK, TOK), 1)
    row = lax.broadcasted_iota(jnp.int32, (TOK, TOK), 0)
    owner = [route[0:1, :], route[1:2, :]]
    number = lax.broadcasted_iota(jnp.int32, (Z * Y, TOK), 0)
    hits = [jnp.where(number == one, 1.0, 0.0) for one in owner]
    earlier = jnp.where(row < lane, 1.0, 0.0).astype(BF16)
    ranks = [jnp.dot(hit.astype(BF16), earlier, preferred_element_type=F32) for hit in hits]
    ranks[1] = ranks[1] + jnp.sum(hits[0], axis=1, keepdims=True)
    ranks = [
        jnp.sum(hit * rank, axis=0, keepdims=True).astype(jnp.int32)
        for hit, rank in zip(hits, ranks)
    ]

    slot_ids = lax.broadcasted_iota(jnp.int32, (SLOTS, TOK), 0)
    for to in range(Y):
        total = jnp.zeros((SLOTS, ROWS), F32)
        lanes = []
        for j in range(2):
            here, group = owner[j] % Y == to, owner[j] // Y
            place = jnp.where(here, group * CAP + ranks[j], -1)
            one = jnp.where(slot_ids == place, 1.0, 0.0).astype(BF16)
            ps[j, pl.ds(to * SLOTS, SLOTS), :] = one
            total = total + lax.dot_general(
                one, dense_t[pl.ds(j * ROWS, ROWS), :], NT, preferred_element_type=F32
            )
            spot = group * (2 * CAP) + ranks[j] + (y % 2) * CAP
            lanes.append(jnp.where(here, spot, -1).astype(F32))
        wm[to, pl.ds(0, SLOTS), :] = total.astype(BF16)
        wm[to, pl.ds(SLOTS, 16), :] = jnp.broadcast_to(
            jnp.concatenate(lanes, axis=1), (16, ROWS)
        ).astype(BF16)
    for dy in (1, 3, 2):
        send(wm.at[(y + dy) % Y], wa.at[c, y], w1[dy], dev(dy=dy))
    wa[c, y] = wm[y]
    w_piece(0)

    c_step(3)
    z_step(2, 0)
    c_step(5)
    y_step(0)
    y_step(1)
    z_step(2, 1)
    c_step(6)
    c_step(7)
    w_piece(1)
    w_piece(3)
    z_step(3, 0)
    w_piece(2)
    y_step(2)
    z_step(3, 1)
    y_step(4)
    w_pass(1, 0)
    w_pass(3, 0)
    w_pass(2, 0)
    z_step(4, 0)
    y_step(3)
    w_last(0)
    z_step(4, 1)
    y_step(5)

    def prepare(i):
        src = source(i)

        def half(yp, carry):
            pi = (src % K) * 8 + (src // K) * 2 + yp
            slots = lax.broadcasted_iota(jnp.int32, (ROWS, TOK), 0).astype(F32)
            at = pl.multiple_of(pi * 16, 16)
            parts = []
            for q in range(2):
                row = wa[src, yp * 2 + q, pl.ds(SLOTS, 16), :].astype(F32)[0:1, :]
                hit = jnp.where(slots == row[:, :TOK], 1.0, 0.0)
                hit = hit + jnp.where(slots == row[:, TOK:], 1.0, 0.0)
                pm[pi, :, pl.ds(q * TOK, TOK)] = hit.astype(BF16)
                part = wa[src, yp * 2 + q, pl.ds(0, SLOTS), :].astype(F32)
                parts.append(part.reshape(Z, CAP, ROWS))
            wt[:, pl.ds(at, 16), :] = jnp.concatenate(parts, axis=1).astype(BF16)
            return carry

        lax.fori_loop(0, 2, half, 0)

    def gather(i):
        src = source(i)

        def half(yp, carry):
            pi = (src % K) * 8 + (src // K) * 2 + yp
            at = pl.multiple_of(pi * 16, 16)
            tokens = oga[src, pl.ds(yp * 2, 2)].reshape(2 * TOK, FEAT)
            got = jnp.dot(pm[pi], tokens, preferred_element_type=F32)
            gt[:, pl.ds(at, 16), :] = got.astype(BF16).reshape(Z, 16, FEAT)
            return carry

        lax.fori_loop(0, 2, half, 0)

    def p_step(s):
        def side(u, carry):
            at = (z + Z + (1 - 2 * u) * s) % Z
            rows = va[at].reshape(ROWS, FEAT)
            pt[at] = jnp.dot(wt[at], rows, preferred_element_type=F32).astype(BF16)
            return carry

        lax.fori_loop(0, 1 if s in (0, 8) else 2, side, 0)

    rid = ids.take(32)

    def grad_part(at, h):
        rows = pl.ds(h * HALF, HALF)
        return lax.dot_general(wt[at, :, rows], gt[at], TN, preferred_element_type=F32)

    def r_step(s, h):
        def stream(way, carry):
            at = (z + Z + (1 - 2 * way) * (8 - s)) % Z
            total = grad_part(at, h)
            if s >= 2:
                arrived(rz.at[s - 1, way, h], rid + (s - 1) * 4 + way * 2 + h)
                total = total + rz[s - 1, way, h].astype(F32)
            sz[s, way, h] = total.astype(BF16)
            if s == 1:

                @pl.when(way == h)
                def _():
                    arrived(rz.at[0, way, h], rid + way * 2 + h)
                    more = total + rz[0, way, h].astype(F32)
                    sz[s, way, h] = more.astype(BF16)

            to_mem = ((z + Z + 1 - 2 * way) % Z) * Y + y
            copy(
                sz.at[s, way, h], rz.at[s, way, h], rid + s * 4 + way * 2 + h, (dp, to_mem)
            ).start()
            return carry

        if s == 0:
            stream(h, 0)
        else:
            lax.fori_loop(0, 2, stream, 0)

    def r_last(h):
        total = grad_part(z, h)
        for way in range(2):
            arrived(rz.at[7, way, h], rid + 28 + way * 2 + h)
            total = total + rz[7, way, h].astype(F32)
        gv_v[pl.ds(h * HALF, HALF), :] = total
        part = pl.ds(h * HALF, HALF)
        done = pltpu.make_async_copy(gv_v.at[part], gv.at[part], lsem.at[h])
        done.start()
        return done

    def r_drain(first, last):
        def drain(i, carry):
            block = sz.at[i // 4, (i // 2) % 2, i % 2]

            @pl.when((i != 1) & (i != 2))
            def _():
                copy(block, block, rid + i, dev(dz=1)).wait_send()

            return carry

        lax.fori_loop(first, last, drain, 0)

    i1 = ids.take()
    i2 = [ids.take() for _ in range(4)]
    i3 = [ids.take() for _ in range(4)]
    m1r = [ids.take() for _ in range(4)]
    m1l = [ids.take() for _ in range(4)]
    mr = [ids.take() for _ in range(8)]
    ml = [ids.take() for _ in range(8)]
    oid = [ids.take() for _ in order]
    far, up, down = (y + 2) % Y, (y + 1) % Y, (y + Y - 1) % Y
    couples = [(6, 7), (2, 3), (4, 5), (0, 1)]

    def to_of(i):
        dx, dk = order[i]
        return cof(dx, dk)

    def scatter(i):
        src = to_of(i)

        def half(yp, carry):
            pi = (src % K) * 8 + (src // K) * 2 + yp
            at = pl.multiple_of(pi * 16, 16)
            parts = pt[:, pl.ds(at, 16), :].reshape(ROWS, FEAT)
            got = lax.dot_general(pm[pi], parts, TN, preferred_element_type=F32)
            outp[src, pl.ds(yp * 2, 2)] = got.astype(BF16).reshape(2, TOK, FEAT)
            return carry

        lax.fori_loop(0, 2, half, 0)

    def m_first(n):
        e, o = couples[n]
        scatter(e)
        send(outp.at[to_of(e), far], ytr.at[n], m1r[n], dev(dy=1))
        send(outp.at[to_of(e), down], yfl.at[e], ml[e], dev(dy=Y - 1))
        scatter(o)
        send(outp.at[to_of(o), far], ytl.at[n], m1l[n], dev(dy=Y - 1))
        send(outp.at[to_of(o), up], yfr.at[o], mr[o], dev(dy=1))

    def m_second(n):
        e, o = couples[n]
        at = to_of(e)
        arrived(ytr.at[n], m1r[n])
        outp[at, up] = (outp[at, up].astype(F32) + ytr[n].astype(F32)).astype(BF16)
        send(outp.at[at, up], yfr.at[e], mr[e], dev(dy=1))
        at = to_of(o)
        arrived(ytl.at[n], m1l[n])
        outp[at, down] = (outp[at, down].astype(F32) + ytl[n].astype(F32)).astype(BF16)
        send(outp.at[at, down], yfl.at[o], ml[o], dev(dy=Y - 1))

    def m_final(n):
        for i in couples[n]:
            dx, dk = order[i]
            to = to_of(i)
            arrived(yfr.at[i], mr[i])
            arrived(yfl.at[i], ml[i])
            total = outp[to, y].astype(F32) + yfr[i].astype(F32) + yfl[i].astype(F32)
            outp[to, y] = total.astype(BF16)
            if i == 0:
                own = pltpu.make_async_copy(outp.at[to, y], out.at[:, cols(c)], lsem.at[3])
                own.start()
                own.wait()
            else:
                send(outp.at[to, y], out.at[:, cols(c)], oid[i], dev(dx=dx, dk=dk))

    def inner(at, carry):
        rows = va[at].reshape(ROWS, FEAT)
        got = lax.dot_general(gt[at], rows, NT, preferred_element_type=F32)
        ip[:, :, at] = got.astype(BF16).reshape(K, X, 32, ROWS)
        return carry

    def add_core(i, carry):
        xx = i // 4
        at = pl.ds((i % 4) * 4, 4)
        ic[xx, at] = (ip[k, xx, at].astype(F32) + ir[xx, at].astype(F32)).astype(BF16)
        return carry

    def add_chips(at, carry):
        total = ic[x, at].astype(F32)
        for i in range(3):
            total = total + ix[i, at].astype(F32)
        for q in range(4):
            iy[q, at] = total[q * CAP : (q + 1) * CAP, :]
        return carry

    for dy in (1, 3, 2):
        w_pass(1, dy)
        w_pass(3, dy)
    z_step(5, 0)
    for dy in (1, 3, 2):
        w_pass(2, dy)
    for one in own_v:
        one.wait()
    own_og.wait()
    prepare(0)
    prepare(1)
    y_step(6)
    y_step(7)
    z_step(5, 1)
    prepare(2)
    prepare(4)
    y_last(0)
    gather(0)
    y_last(1)
    gather(1)
    z_step(6, 0)
    prepare(6)
    w_last(1)
    w_last(3)
    prepare(3)
    prepare(5)
    y_last(2)
    gather(2)
    w_last(2)
    prepare(7)
    z_step(6, 1)
    for step in range(4):
        p_step(step)
    y_last(3)
    gather(3)
    y_last(4)
    gather(4)
    z_step(7, 0)
    p_step(4)
    p_step(5)
    y_last(5)
    gather(5)
    for i in (6, 7):
        y_last(i)
        gather(i)
    r_step(0, 0)
    z_step(7, 1)
    r_step(0, 1)
    p_step(6)
    z_step(8, 0)
    p_step(7)
    z_step(8, 1)
    p_step(8)
    early = len(sent)
    m_first(0)
    m_first(1)
    r_step(1, 0)
    r_step(1, 1)
    lax.fori_loop(0, Z // 2, inner, 0)
    r_step(2, 0)
    m_second(0)
    m_first(2)
    r_step(2, 1)
    lax.fori_loop(Z // 2, Z, inner, 0)
    send(ip.at[(k + 1) % K], ir, i1, dev(dk=1))
    r_step(3, 0)
    m_second(1)
    m_first(3)
    r_step(3, 1)
    arrived(ir, i1)
    lax.fori_loop(0, 16, add_core, 0)
    for dx in (1, 3, 2):
        send(ic.at[(x + dx) % X], ix.at[dx - 1], i2[dx], dev(dx=dx))
    r_step(4, 0)
    m_final(0)
    r_step(4, 1)
    m_second(2)
    r_step(5, 0)
    for one in sent[: early // 2]:
        one.wait_send()
    del sent[: early // 2]
    early -= early // 2
    r_step(5, 1)
    m_final(1)
    r_step(6, 0)
    m_second(3)
    for dx in (1, 3, 2):
        arrived(ix.at[dx - 1], i2[dx])
    lax.fori_loop(0, Z, add_chips, 0)
    for q in range(4):
        isrc[4, pl.ds(q * SLOTS, SLOTS), :] = iy[q].reshape(SLOTS, ROWS).astype(BF16)
    isrc[0, pl.ds(0, SLOTS), :] = isrc[4, pl.ds(pl.multiple_of(y * SLOTS, SLOTS), SLOTS), :]
    for i in range(1, 4):
        to = (y + i) % Y
        send(
            isrc.at[4, pl.ds(pl.multiple_of(to * SLOTS, SLOTS), SLOTS), :],
            isrc.at[i, pl.ds(0, SLOTS), :], i3[i], dev(dy=i),
        )
    r_step(6, 1)
    for one in sent[:early]:
        one.wait_send()
    del sent[:early]
    r_drain(0, 20)
    r_step(7, 0)
    m_final(2)
    r_step(7, 1)
    for i in range(1, 4):
        arrived(isrc.at[i, pl.ds(0, SLOTS), :], i3[i])
    for j in range(2):
        total = jnp.zeros((TOK, ROWS), F32)
        for i in range(4):
            at = pl.multiple_of(((y + Y - i) % Y) * SLOTS, SLOTS)
            total = total + lax.dot_general(
                ps[j, pl.ds(at, SLOTS), :], isrc[i, pl.ds(0, SLOTS), :], TN,
                preferred_element_type=F32,
            )
        pair_v[:, pl.ds(j * ROWS, ROWS)] = total
    pair_out = pltpu.make_async_copy(pair_v, pair, lsem.at[6])
    pair_out.start()
    m_final(3)
    gv_done = [r_last(0)]
    for i in range(1, 8):
        arrived(out.at[:, cols(source(i))], oid[i])
    gv_done.append(r_last(1))
    pair_out.wait()
    for one in sent:
        one.wait_send()
    r_drain(20, 32)
    for one in gv_done:
        one.wait()
    assert ids.count <= SEMS, ids.count


SEMS = 192


def pick(
    pair_in, slot_in, out_in, gv_in, out_ref, out_out, gv_out,
    pair_v, slot_v, picked, out_v, gv_v, fetch_sem, put_sem,
):
    number = 8
    blocks = [(pair_in, pair_v, None), (slot_in, slot_v, None)]
    for n in range(number):
        part = pl.ds(n * TOK // number, TOK // number)
        blocks.append((out_in.at[part], out_v.at[part], out_out.at[part]))
    for n in range(4):
        part = pl.ds(n * ROWS // 4, ROWS // 4)
        blocks.append((gv_in.at[part], gv_v.at[part], gv_out.at[part]))
    fetch = [
        pltpu.make_async_copy(src, held, fetch_sem.at[n])
        for n, (src, held, _) in enumerate(blocks)
    ]
    put = [
        pltpu.make_async_copy(held, dst, put_sem.at[n])
        for n, (_, held, dst) in enumerate(blocks)
        if dst is not None
    ]
    for one in fetch:
        one.start()
    fetch[0].wait()
    fetch[1].wait()
    slot = slot_v[...].T
    low, high = slot & 127, slot // 128
    total = jnp.zeros((TOK, PICKS), F32)
    for a in range(4):
        part = jnp.take_along_axis(pair_v[:, pl.ds(a * 128, 128)], low, axis=1)
        total = jnp.where(high == a, part, total)
    picked[...] = total.T
    last = pltpu.make_async_copy(picked, out_ref, put_sem.at[0])
    last.start()
    for one, two in zip(fetch[2:], put):
        one.wait()
        two.start()
    for one in put:
        one.wait()
    last.wait()


def shards(lookup_slot, lookup_weight, owner_route, values, out_grad):
    slot_t = lookup_slot.transpose(1, 2, 0).reshape(PICKS, TOK)
    weight_t = lookup_weight.transpose(1, 2, 0).reshape(PICKS, TOK)
    hbm = pl.BlockSpec(memory_space=pltpu.HBM)
    vmem, anywhere = pl.BlockSpec(memory_space=pltpu.VMEM), pl.BlockSpec(memory_space=pl.ANY)
    out, gv, pair = pl.pallas_call(
        exchange,
        out_shape=(
            jax.ShapeDtypeStruct((TOK, C * FEAT), BF16),
            jax.ShapeDtypeStruct((ROWS, FEAT), F32),
            jax.ShapeDtypeStruct((TOK, 2 * ROWS), F32),
        ),
        in_specs=[anywhere] * 5,
        out_specs=(anywhere, anywhere, anywhere),
        scratch_shapes=[
            pltpu.VMEM((Z, 2, HALF, FEAT), BF16),
            pltpu.VMEM((C, Y, TOK, FEAT), BF16),
            pltpu.VMEM((Y, MSG, ROWS), BF16),
            pltpu.VMEM((C, Y, MSG, ROWS), BF16),
            pltpu.VMEM((2, Y * SLOTS, TOK), BF16),
            pltpu.VMEM((2 * ROWS, TOK), BF16),
            pltpu.VMEM((PICKS, TOK), jnp.int32),
            pltpu.VMEM((PICKS, TOK), F32),
            pltpu.VMEM((2, TOK), jnp.int32),
            pltpu.VMEM((TOK, 2 * ROWS), F32),
            pltpu.VMEM((ROWS, FEAT), F32),
            pltpu.VMEM((16, ROWS, 2 * TOK), BF16),
            pltpu.VMEM((Z, 16 * 16, ROWS), BF16),
            pltpu.VMEM((Z, 16 * 16, FEAT), BF16),
            pltpu.VMEM((Z, 16 * 16, FEAT), BF16),
            pltpu.VMEM((K, X, Z, 32, ROWS), BF16),
            pltpu.VMEM((X, Z, 32, ROWS), BF16),
            pltpu.VMEM((X, Z, 32, ROWS), BF16),
            pltpu.VMEM((3, Z, 32, ROWS), BF16),
            pltpu.VMEM((4, Z, CAP, ROWS), F32),
            pltpu.VMEM((5, Y * SLOTS, ROWS), BF16),
            pltpu.VMEM((C, Y, TOK, FEAT), BF16),
            pltpu.VMEM((4, TOK, FEAT), BF16),
            pltpu.VMEM((4, TOK, FEAT), BF16),
            pltpu.VMEM((C, TOK, FEAT), BF16),
            pltpu.VMEM((C, TOK, FEAT), BF16),
            pltpu.VMEM((8, 2, 2, HALF, FEAT), BF16),
            pltpu.VMEM((8, 2, 2, HALF, FEAT), BF16),
            pltpu.SemaphoreType.DMA((SEMS,)),
            pltpu.SemaphoreType.DMA((SEMS,)),
            pltpu.SemaphoreType.DMA((8,)),
        ],
        compiler_params=pltpu.CompilerParams(
            collective_id=0, has_side_effects=True, vmem_limit_bytes=58 * 1024 * 1024
        ),
        name="exchange",
    )(slot_t, weight_t, owner_route.T, out_grad, values)
    grad_weight, out, gv = pl.pallas_call(
        pick,
        out_shape=(
            jax.ShapeDtypeStruct((PICKS, TOK), F32),
            jax.ShapeDtypeStruct(out.shape, out.dtype),
            jax.ShapeDtypeStruct(gv.shape, gv.dtype),
        ),
        in_specs=[hbm] * 4,
        out_specs=(hbm, hbm, hbm),
        scratch_shapes=[
            pltpu.VMEM((TOK, 2 * ROWS), F32),
            pltpu.VMEM((PICKS, TOK), jnp.int32),
            pltpu.VMEM((PICKS, TOK), F32),
            pltpu.VMEM((TOK, C * FEAT), BF16),
            pltpu.VMEM((ROWS, FEAT), F32),
            pltpu.SemaphoreType.DMA((14,)),
            pltpu.SemaphoreType.DMA((14,)),
        ],
        name="pick",
    )(pair, slot_t, out, gv)
    return out, gv, grad_weight.reshape(4, 32, TOK).transpose(2, 0, 1)


def solution(mesh):
    return jax.shard_map(
        shards,
        mesh=mesh,
        in_specs=(
            P(("dp", "mem"), None, None),
            P(("dp", "mem"), None, None),
            P(("dp", "mem"), None),
            P("mem", None),
            P(("dp", "mem"), None),
        ),
        out_specs=(P(("dp", "mem"), None), P("mem", "dp"), P(("dp", "mem"), None, None)),
        check_vma=False,
    )
```
